512 devices in a mesh: group: 64 (over z, x, core), tp: 8 (over y).
Axes of the slice: x: 4, y: 8, z: 8, core: 2. Of those that a mesh axis runs over, the one named last changes fastest.
Arguments:
- saved: bfloat16 [128, 128, 5120], P('group'), may hold values from -400 to 400
- block_per_slot: int32 [128], P('group'), may hold values from 0 to 127, each once
- lengths: int32 [4], replicated, may hold values from 1 to 4096, 8192 in all
- norm_gain: bfloat16 [5120], replicated, may hold values from 0.099609375 to 1.8984375
- kv_weight: bfloat16 [5120, 2, 5120], P('group', None, 'tp'), may hold values from -0.078125 to 0.078125
- out_weight: bfloat16 [5120, 5120], P('tp', 'group'), may hold values from -0.078125 to 0.078125
- queries: bfloat16 [64, 5120], P('group', 'tp'), may hold values from -400 to 400
- new_kv: bfloat16 [64, 2, 5120], P('group', None, 'tp'), may hold values from -6 to 6
- row_conv: int32 [64], P('group'), may hold values from 0 to 3
Outputs:
- kv_cache: bfloat16 [128, 128, 2, 5120], P('group', None, None, 'tp')
- decoded: bfloat16 [64, 5120], P('tp', 'group')
The draws below stay inside these ranges and needn't reach their ends.
Inputs may be any that keep to these rules, and one draw needn't show every extreme that they name: `block_per_slot`: every block number 0 to 128 - 1 (conversation c, block b as c * 32 + b) is held by exactly one slot. The lengths sum to 8192; the longest is 4096.
All inputs are finite; a program needn't handle non-finite values.
Results may differ from the reference program's by a relative error of at most 0.019.
Values may be sent and summed in bfloat16 or wider, within the bound.
No kernel may reach another device: no remote copies, remote signals or barrier semaphores. Data moves between devices by JAX's collectives and lax.ppermute only.
A program may use at most 128 MiB of HBM per device.

```python
import math
import jax
import jax.numpy as jnp
import numpy as np
from jax import lax

MODEL_DIMENSION = 5120
HEADS = 40
HEAD_DIM = 128
SAVED_BLOCK_ROWS = 128
CONV = 4
SLOT_COUNT = 128
NBLK = 32
MAXLEN = 4096
ROWS = 64


def draw_saved(key, part):
    key = jax.random.fold_in(key, 11)
    first_key, latter_key, third_key = jax.random.split(key, 3)
    draw_shape = (SLOT_COUNT, SAVED_BLOCK_ROWS, MODEL_DIMENSION)
    col_scale = jnp.exp(jax.random.uniform(third_key, (1, 1, MODEL_DIMENSION), jnp.float32, 0.0, math.log(10.0)))
    base_draw = jax.random.truncated_normal(first_key, -4.0, 4.0, draw_shape, jnp.float32)
    scale_per_row = jnp.exp(jax.random.uniform(latter_key, (SLOT_COUNT, SAVED_BLOCK_ROWS, 1), jnp.float32, 0.0, math.log(10.0)))
    return (base_draw * scale_per_row * col_scale).astype(jnp.bfloat16)


def draw_queries(key, part):
    key = jax.random.fold_in(key, 23)
    draw_shape = (ROWS, HEADS * HEAD_DIM)
    return (2.5 * jax.random.truncated_normal(key, -4.0, 4.0, draw_shape, jnp.float32)).astype(jnp.bfloat16)


def with_ends(array, key, least, high):
    dims = array.shape
    spot = [jax.random.randint(jax.random.fold_in(key, axis), (), 0, dims[axis]) for axis in range(len(dims))]
    array = array.at[tuple(spot)].set(least)
    longest = dims.index(max(dims))
    spot[longest] = (spot[longest] + 1) % dims[longest]
    return array.at[tuple(spot)].set(high)


def block_levels(key, dims, shards, smallest, largest):
    factor_of = 1.0
    for axis_at, shards_of in shards:
        heights = jax.random.uniform(jax.random.fold_in(jax.random.fold_in(key, 6), axis_at), (shards_of,), jnp.float32, smallest / len(shards), largest / len(shards))
        factor_of = factor_of * jnp.repeat(jnp.exp(heights), dims[axis_at] // shards_of).reshape((-1,) + (1,) * (len(dims) - 1 - axis_at))
    return factor_of


def split_up(amount, total, limit, skew):
    weights = [(1 << 20) // math.isqrt(standing ** skew) + 1 for standing in range(2, amount + 1)]
    surplus, holding = total - limit - (amount - 1), [1] * (amount - 1)
    while surplus > 0:
        movable = [i for i in range(amount - 1) if holding[i] < limit]
        whole, budget = sum([weights[i] for i in movable]), surplus
        for i in movable:
            addition = min(limit - holding[i], max(1, budget * weights[i] // whole), surplus)
            holding[i] = holding[i] + addition
            surplus = surplus - addition
    return np.array([limit] + holding)


def ragged(key, count, total, most, lean):
    if count == 2:
        one = jax.random.randint(key, (), max(1, total - most), min(most, total - 1) + 1)
        return jnp.stack([one, total - one])
    sizes = jnp.asarray(split_up(count, total, most, lean), jnp.int32)
    twos = (count - 1) // 2
    source_of, receiver = sizes[1:1 + 2 * twos:2], sizes[2:2 + 2 * twos:2]
    slack = jnp.minimum(source_of - 1, most - receiver)
    passed = jax.random.randint(jax.random.fold_in(key, 1), (twos,), 0, 1 << 20) % (slack + 1)
    sizes = sizes.at[1:1 + 2 * twos:2].set(source_of - passed).at[2:2 + 2 * twos:2].set(receiver + passed)
    return sizes[jax.random.permutation(jax.random.fold_in(key, 2), count)]


def noise(stream_key, extent, spread, most, cuts=(), held_as=jnp.bfloat16):
    values = jax.random.normal(stream_key, extent, jnp.float32) * spread
    if len(cuts) > 0:
        values = block_levels(stream_key, extent, cuts, -0.22, 0.18) * values
    return jnp.clip(values, min=-most, max=most).astype(held_as)


def setup_inputs(seed: int = 0) -> dict:
    arg_keys = jax.random.split(jax.random.key(seed), 10)
    return {
        "saved": draw_saved(jax.random.fold_in(arg_keys[9], 71), 0),
        "block_per_slot": jax.random.permutation(arg_keys[1], SLOT_COUNT).astype(jnp.int32),
        "lengths": ragged(arg_keys[2], CONV, 2 * MAXLEN, MAXLEN, 0).astype(jnp.int32),
        "norm_gain": jnp.clip(1.0 + 0.18 * jax.random.normal(arg_keys[3], (MODEL_DIMENSION,), jnp.float32), 0.099609375, 1.8984375).astype(jnp.bfloat16),
        "kv_weight": noise(arg_keys[4], (MODEL_DIMENSION, 2, HEADS * HEAD_DIM), MODEL_DIMENSION ** -0.5, 0.078125, ((0, 64), (2, 8))),
        "out_weight": noise(arg_keys[5], (HEADS * HEAD_DIM, MODEL_DIMENSION), (HEADS * HEAD_DIM) ** -0.5, 0.078125, ((0, 8), (1, 64))),
        "queries": draw_queries(jax.random.fold_in(arg_keys[9], 71), 0),
        "new_kv": noise(arg_keys[7], (ROWS, 2, HEADS * HEAD_DIM), 1.0, 6.0, ((0, 64), (2, 8))),
        "row_conv": with_ends(jax.random.randint(arg_keys[8], (ROWS,), 0, CONV), jax.random.fold_in(arg_keys[8], 1), 0, CONV - 1).astype(jnp.int32),
    }


EPSILON = 1e-05
NEG_FILL = -1e+30

def rotate(key_heads, positions):
    half_dim = key_heads.shape[-1] // 2
    freq_index = jnp.arange(half_dim, dtype=jnp.float32)
    inverse = jnp.exp(freq_index * (-2.0 * math.log(10000.0) / key_heads.shape[-1]))
    angles = positions.astype(jnp.float32)[..., None] * inverse
    cosine = jnp.cos(angles)[..., None, :]
    sine_part = jnp.sin(angles)[..., None, :]
    first_half = key_heads[..., :half_dim]
    second = key_heads[..., half_dim:]
    return jnp.concatenate([first_half * cosine - second * sine_part, second * cosine + first_half * sine_part], axis=-1)

def finish(projected, positions, row_live, kv_width):
    lead_shape = projected.shape[:-1]
    key_heads = projected[..., :kv_width].reshape(lead_shape + (kv_width // HEAD_DIM, HEAD_DIM))
    rotated = rotate(key_heads, positions).reshape(lead_shape + (kv_width,))
    values = projected[..., kv_width:]
    stacked = jnp.stack([rotated, values], axis=-2)
    return jnp.where(row_live[..., None, None], stacked, 0.0).astype(jnp.bfloat16)

def normalize(saved_rows, norm_gain):
    as_float = saved_rows.astype(jnp.float32)
    inv_rms = lax.rsqrt(lax.optimization_barrier(jnp.mean(as_float * as_float, axis=-1, keepdims=True)) + EPSILON)
    return (as_float * inv_rms * norm_gain.astype(jnp.float32)).astype(jnp.bfloat16)

def reference(saved, block_per_slot, lengths, norm_gain, kv_weight, out_weight, queries, new_kv, row_conv):
    kv_width = HEADS * HEAD_DIM
    conv_of = (block_per_slot // NBLK).astype(jnp.int32)
    start_of = block_per_slot % NBLK * SAVED_BLOCK_ROWS
    positions = start_of[:, None] + jnp.arange(SAVED_BLOCK_ROWS, dtype=jnp.int32)[None, :]
    row_mask = positions < lengths[conv_of][:, None]
    weight_columns = kv_weight.reshape(MODEL_DIMENSION, 2 * kv_width)

    def restore(slot_item):
        slot_rows, slot_pos, slot_live = slot_item

        def project_slot(unused):
            projected = jnp.dot(normalize(slot_rows, norm_gain), weight_columns, preferred_element_type=jnp.float32)
            return finish(projected, slot_pos, slot_live, kv_width)

        def zero_slot(unused):
            return jnp.zeros((SAVED_BLOCK_ROWS, 2, kv_width), jnp.bfloat16)
        return lax.cond(jnp.any(slot_live), project_slot, zero_slot, 0)
    kv_cache = lax.map(restore, (saved, positions, row_mask))
    inv_sqrt = 1.0 / math.sqrt(HEAD_DIM)
    query_heads = queries.astype(jnp.float32).reshape(ROWS, HEADS, HEAD_DIM)
    own_key = new_kv[:, 0].astype(jnp.float32).reshape(ROWS, HEADS, HEAD_DIM)
    own_value = new_kv[:, 1].astype(jnp.float32).reshape(ROWS, HEADS, HEAD_DIM)
    own_score = lax.optimization_barrier(jnp.sum(query_heads * own_key, axis=-1)) * inv_sqrt
    slot_of = jnp.argsort(block_per_slot).astype(jnp.int32)
    attended = jnp.zeros((ROWS, kv_width), jnp.float32)
    for chat_index in range(CONV):
        slot_list = slot_of[chat_index * NBLK:(chat_index + 1) * NBLK]
        block_kv = kv_cache[slot_list].reshape(MAXLEN, 2, HEADS, HEAD_DIM)
        cache_keys = block_kv[:, 0].astype(jnp.float32)
        cache_values = block_kv[:, 1].astype(jnp.float32)
        key_valid = jnp.arange(MAXLEN, dtype=jnp.int32) < lengths[chat_index]
        scores = jnp.einsum('rhd,khd->rhk', query_heads, cache_keys) * inv_sqrt
        row_top = jnp.maximum(lax.optimization_barrier(jnp.max(jnp.where(key_valid, scores, NEG_FILL), axis=-1)), own_score)
        attn_weight = jnp.where(key_valid, jnp.exp(scores - row_top[..., None]), 0.0).astype(jnp.bfloat16)
        attn_weight = lax.optimization_barrier(attn_weight).astype(jnp.float32)
        own_weight = lax.optimization_barrier(jnp.exp(own_score - row_top).astype(jnp.bfloat16)).astype(jnp.float32)
        weight_sum = lax.optimization_barrier(jnp.sum(attn_weight, axis=-1)) + own_weight
        weighted = jnp.einsum('rhk,khd->rhd', attn_weight, cache_values) + own_weight[..., None] * own_value
        result = (weighted / weight_sum[..., None]).reshape(ROWS, kv_width)
        attended = jnp.where((row_conv == chat_index)[:, None], result, attended)
    attended = attended.astype(jnp.bfloat16)
    decoded = jnp.dot(attended, out_weight, preferred_element_type=jnp.float32).astype(jnp.bfloat16)
    return (kv_cache, decoded)
```

```python
import functools
import math

import jax
import jax.numpy as jnp
from jax import lax
from jax.experimental import pallas as pl
from jax.experimental.pallas import tpu as pltpu
from jax.sharding import Mesh
from jax.sharding import PartitionSpec as P

HEAD_DIM = 128
EPSILON = 1e-05
NEG_FILL = -1e30
GROUP = ("z", "x", "core")
MIB = 1 << 20
Z_CHIPS, X_CHIPS = 8, 4
Z_RING, X_RING = (0, -1, 1, -2, 2, -3, 3, 4), (0, -1, 1, 2)
TOP_PARTS, SUM_PARTS = 3, 2


def normalize(saved_rows, norm_gain):
    as_float = saved_rows.astype(jnp.float32)
    inv_rms = lax.rsqrt(jnp.mean(as_float * as_float, axis=-1, keepdims=True) + EPSILON)
    return (as_float * inv_rms * norm_gain.astype(jnp.float32)).astype(jnp.bfloat16)


def lookup(lookup_table, indices):
    matches = indices[..., None] == jnp.arange(lookup_table.shape[0], dtype=jnp.int32)
    return jnp.sum(jnp.where(matches, lookup_table, 0), axis=-1)


def swap_cores(value):
    return lax.ppermute(value, "core", [(0, 1), (1, 0)])


def chip_of(place_ref, dz, dx):
    sign = 1 - 2 * place_ref[2]
    z = lax.rem(place_ref[0] + sign * dz + Z_CHIPS, Z_CHIPS)
    x = lax.rem(place_ref[1] + sign * dx + X_CHIPS, X_CHIPS)
    return z * X_CHIPS + x


def project_kernel(split, place_ref, own_ref, other_ref, cos_ref, sin_ref, *refs):
    a_refs, b_refs = refs[: len(X_RING)], refs[len(X_RING) : len(X_RING) + len(Z_RING)]
    own_out, other_out, query_out, weight = refs[len(X_RING) + len(Z_RING) :]
    core = place_ref[2]
    rows, depth = own_ref.shape
    width = weight.shape[1]
    half = depth // (2 * Z_CHIPS * X_CHIPS)
    extra = a_refs[0].shape[0] // len(Z_RING) - 2 * half

    def place(piece, at, chip, columns):
        for part, whose in ((0, core), (1, 1 - core)):
            to = pl.multiple_of((2 * chip + whose) * half, 16)
            weight[pl.ds(to, half), columns] = piece[pl.ds(at + part * half, half), :]

    for i, dx in enumerate(X_RING):
        for j, dz in enumerate(Z_RING):
            chip = chip_of(place_ref, dz, dx)
            at = j * (2 * half + extra)
            place(a_refs[i], at, chip, pl.ds(0, split))
            tiles = a_refs[i][pl.ds(at + 2 * half, extra), :].astype(jnp.float32)
            query_out[chip, pl.ds(pl.multiple_of(core * 8, 8), 8), :] = tiles[:8]
            query_out[chip, pl.ds(pl.multiple_of(8 - core * 8, 8), 8), :] = tiles[8:16]
            place(b_refs[j], i * 2 * half, chip, pl.ds(split, width - split))

    chunk = 1024 if depth % 1024 == 0 else depth
    for part, (rows_ref, out) in enumerate(((own_ref, own_out), (other_ref, other_out))):
        span = pl.ds(part * rows, rows)
        total = jnp.zeros((rows, width), jnp.float32)
        for k in range(depth // chunk):
            lanes = pl.ds(k * chunk, chunk)
            total += jnp.dot(
                rows_ref[:, lanes], weight[lanes, :], preferred_element_type=jnp.float32
            )
        cosine, sine = cos_ref[span, :], sin_ref[span, :]
        for head in range(width // HEAD_DIM):
            value = total[:, head * HEAD_DIM : (head + 1) * HEAD_DIM]
            turned = value * cosine + pltpu.roll(value, HEAD_DIM // 2, 1) * sine
            out[:, pl.ds(head * HEAD_DIM, HEAD_DIM)] = turned.astype(out.dtype)


def project(place, own, other, cosine, sine, a_blocks, b_blocks):
    rows, depth = own.shape
    split = a_blocks[0].shape[1]
    width = split + b_blocks[0].shape[1]
    out = jax.ShapeDtypeStruct((rows, width), jnp.bfloat16)
    tiles = jax.ShapeDtypeStruct((Z_CHIPS * X_CHIPS, 16, split), jnp.float32)
    vmem = pl.BlockSpec(memory_space=pltpu.VMEM)
    operands = (own, other, cosine, sine, *a_blocks, *b_blocks)
    return pl.pallas_call(
        functools.partial(project_kernel, split),
        in_specs=[pl.BlockSpec(memory_space=pltpu.SMEM)] + [vmem] * len(operands),
        out_specs=[vmem] * 3,
        out_shape=[out, out, tiles],
        scratch_shapes=[pltpu.VMEM((depth, width), jnp.bfloat16)],
        compiler_params=pltpu.CompilerParams(vmem_limit_bytes=40 * MIB),
        cost_estimate=pl.CostEstimate(
            flops=4 * rows * depth * width,
            bytes_accessed=4 * rows * depth + 2 * depth * width,
            transcendentals=0,
        ),
    )(place, *operands)


def attend_kernel(place_ref, mine_ref, theirs_ref, query_ref, keys_ref, out_ref, tiles):
    has_keys = place_ref[2] == 0
    chips = query_ref.shape[0]
    heads = mine_ref.shape[1] // HEAD_DIM
    key_conv = keys_ref[0:1, :]

    def rows_of(part):
        lanes = pl.ds(part % 2 * HEAD_DIM, HEAD_DIM)
        return jnp.concatenate([query_ref[:, core * 8 + part // 2, lanes] for core in (0, 1)])

    allowed = rows_of(heads)[:, 0:1] == key_conv
    lane = lax.broadcasted_iota(jnp.int32, (2 * chips, HEAD_DIM), 1)
    stats = jnp.zeros(lane.shape, jnp.float32)

    def put(row, value):
        for core in (0, 1):
            tiles[:, core, row, :] = value[core * chips : (core + 1) * chips]

    for head in range(heads):
        lanes = pl.ds(head * HEAD_DIM, HEAD_DIM)
        mine, theirs = mine_ref[:, lanes], theirs_ref[:, lanes]
        keys = jnp.where(has_keys, mine, theirs)
        values = jnp.where(has_keys, theirs, mine)
        scores = lax.dot_general(
            rows_of(head).astype(jnp.bfloat16),
            keys,
            (((1,), (1,)), ((), ())),
            preferred_element_type=jnp.float32,
        )
        scores = jnp.where(allowed, scores * (1.0 / math.sqrt(HEAD_DIM)), NEG_FILL)
        top = jnp.max(scores, axis=-1, keepdims=True)
        weight = jnp.where(allowed, jnp.exp(scores - top), 0.0).astype(jnp.bfloat16)
        total = jnp.sum(weight.astype(jnp.float32), axis=-1, keepdims=True)
        put(head, jnp.dot(weight, values, preferred_element_type=jnp.float32))
        at = head
        for value, parts in ((top, TOP_PARTS), (total, SUM_PARTS)):
            for _ in range(parts):
                rounded = value.astype(jnp.bfloat16).astype(jnp.float32)
                stats = jnp.where(lane == at, rounded, stats)
                value = value - rounded
                at += 8
    put(heads, stats)
    for row in range(heads + 1, 8):
        put(row, jnp.zeros_like(stats))
    out_ref[...] = tiles[...].astype(jnp.bfloat16)


def attend(place, mine, theirs, queries, key_conv):
    shape = (queries.shape[0], 2, 8, HEAD_DIM)
    vmem = pl.BlockSpec(memory_space=pltpu.VMEM)
    return pl.pallas_call(
        attend_kernel,
        in_specs=[pl.BlockSpec(memory_space=pltpu.SMEM)] + [vmem] * 4,
        out_specs=vmem,
        out_shape=jax.ShapeDtypeStruct(shape, jnp.bfloat16),
        scratch_shapes=[pltpu.VMEM(shape, jnp.float32)],
        compiler_params=pltpu.CompilerParams(vmem_limit_bytes=16 * MIB),
    )(place, mine, theirs, queries, key_conv)


def merge_kernel(heads, parts_ref, query_ref, new_ref, out_ref, parts, tile):
    parts[...] = parts_ref[...].astype(jnp.float32)
    stats = parts[:, heads, :]
    tile[...] = jnp.zeros_like(tile)
    for head in range(heads):
        lanes = pl.ds(head * HEAD_DIM, HEAD_DIM)
        query = query_ref[:, lanes].astype(jnp.float32)
        own_key = new_ref[0:1, lanes].astype(jnp.float32)
        own_value = new_ref[1:2, lanes].astype(jnp.float32)
        own = jnp.sum(query * own_key, axis=-1, keepdims=True) * (1.0 / math.sqrt(HEAD_DIM))
        stat = [stats[:, head + 8 * k : head + 8 * k + 1] for k in range(TOP_PARTS + SUM_PARTS)]
        top, total = sum(stat[1:TOP_PARTS], stat[0]), sum(stat[TOP_PARTS + 1 :], stat[TOP_PARTS])
        best = jnp.maximum(jnp.max(top, axis=0, keepdims=True), own)
        factor = jnp.exp(top - best)
        own_weight = jnp.exp(own - best).astype(jnp.bfloat16).astype(jnp.float32)
        total = jnp.sum(total * factor, axis=0, keepdims=True) + own_weight
        mixed = jnp.sum(parts[:, head, :] * factor, axis=0, keepdims=True)
        tile[head : head + 1, :] = (mixed + own_weight * own_value) / total
    out_ref[...] = jnp.broadcast_to(tile[...].astype(jnp.bfloat16), out_ref.shape)


def merge(parts, query, new_pair):
    vmem = pl.BlockSpec(memory_space=pltpu.VMEM)
    return pl.pallas_call(
        functools.partial(merge_kernel, query.shape[1] // HEAD_DIM),
        in_specs=[vmem] * 3,
        out_specs=vmem,
        out_shape=jax.ShapeDtypeStruct(parts.shape, jnp.bfloat16),
        scratch_shapes=[
            pltpu.VMEM(parts.shape, jnp.float32),
            pltpu.VMEM(parts.shape[1:], jnp.float32),
        ],
        compiler_params=pltpu.CompilerParams(vmem_limit_bytes=16 * MIB),
    )(parts, query, new_pair)


def send(value, dz, dx):
    pairs = []
    for z in range(Z_CHIPS):
        for x in range(X_CHIPS):
            for core, sign in ((0, 1), (1, -1)):
                to = ((z + sign * dz) % Z_CHIPS * X_CHIPS + (x + sign * dx) % X_CHIPS) * 2 + core
                pairs.append(((z * X_CHIPS + x) * 2 + core, to))
    return lax.ppermute(value, GROUP, pairs)


def ring(value, chips, dz, dx):
    behind, ahead, found = value, value, [value]
    for _ in range(chips // 2 - 1):
        behind, ahead = send(behind, dz, dx), send(ahead, -dz, -dx)
        found += [behind, ahead]
    return found + [send(behind, dz, dx)]


def exchange(value, axis):
    return lax.all_to_all(value, axis, 0, 0, tiled=True)


def per_device(
    saved, block_per_slot, lengths, norm_gain, kv_weight, out_weight, queries, new_kv, row_conv
):
    slot_dev, block_rows, model_width = saved.shape
    groups = lax.axis_size(GROUP)
    blocks_conv = slot_dev * groups // lengths.shape[0]
    local_width = kv_weight.shape[2]
    heads = local_width // HEAD_DIM
    core = lax.axis_index("core")
    first_core = core == 0

    split = 2 * HEAD_DIM
    keep = jnp.where(first_core, kv_weight[:, 0], kv_weight[:, 1])
    give = jnp.where(first_core, kv_weight[:, 1], kv_weight[:, 0])
    notes = jnp.concatenate(
        [
            queries.reshape(-1),
            jnp.broadcast_to(row_conv.astype(jnp.bfloat16), (HEAD_DIM,)),
            block_per_slot.astype(jnp.bfloat16),
        ]
    )
    notes = jnp.pad(notes, (0, 8 * split - notes.shape[0])).reshape(8, split)
    sent = jnp.concatenate([give, jnp.pad(notes, ((0, 8), (0, local_width - split)))])
    got = swap_cores(sent)
    part_rows = keep.shape[0]
    got_notes = got[part_rows : part_rows + 8, :split]
    piece_a = jnp.concatenate([keep[:, :split], got[:part_rows, :split], notes, got_notes])
    piece_b = jnp.concatenate([keep[:, split:], got[:part_rows, split:]])
    block_b = jnp.concatenate(
        [piece_b, send(piece_b, 0, 1), send(piece_b, 0, -1), send(piece_b, 0, 2)]
    )
    block_a = jnp.concatenate(ring(piece_a, Z_CHIPS, 1, 0))
    b_blocks = ring(block_b, Z_CHIPS, 1, 0)
    a_blocks = ring(block_a, X_CHIPS, 0, 1)

    normed = normalize(saved, norm_gain).reshape(slot_dev * block_rows, model_width)
    other_normed = swap_cores(normed)
    flat = local_width + HEAD_DIM
    other_blocks = got_notes[flat // split, flat % split : flat % split + slot_dev]
    blocks = jnp.concatenate([block_per_slot, other_blocks.astype(jnp.int32)])
    conv = blocks // blocks_conv
    positions = (blocks % blocks_conv * block_rows)[:, None] + jnp.arange(
        block_rows, dtype=jnp.int32
    )
    live = (positions < lookup(lengths, conv)[:, None]).reshape(-1, 1)
    half_dim = HEAD_DIM // 2
    freq_index = jnp.arange(half_dim, dtype=jnp.float32)
    inverse = jnp.exp(freq_index * (-2.0 * math.log(10000.0) / HEAD_DIM))
    angles = positions.reshape(-1, 1).astype(jnp.float32) * inverse
    cosine, sine = jnp.cos(angles), jnp.sin(angles)
    cosine = jnp.where(first_core, jnp.concatenate([cosine, cosine], axis=-1), 1.0)
    sine = jnp.where(first_core, jnp.concatenate([-sine, sine], axis=-1), 0.0)
    cosine, sine = jnp.where(live, cosine, 0.0), jnp.where(live, sine, 0.0)
    own_rows = slot_dev * block_rows
    key_conv = jnp.where(live[:own_rows, 0], jnp.repeat(conv[:slot_dev], block_rows), -1)
    key_conv = jnp.broadcast_to(key_conv.astype(jnp.float32), (8, own_rows))
    place = jnp.stack([lax.axis_index("z"), lax.axis_index("x"), core]).astype(jnp.int32)

    mine, for_other, tiles = project(
        place, normed, other_normed, cosine, sine, a_blocks, b_blocks
    )
    theirs = swap_cores(for_other)
    parts = attend(place, mine, theirs, tiles, key_conv).reshape(groups, 8, HEAD_DIM)
    merged = merge(exchange(parts, GROUP), queries, new_kv[0])
    attended = exchange(merged, GROUP)[:, :heads].reshape(groups, local_width)
    decoded = jnp.dot(attended, out_weight, preferred_element_type=jnp.float32)
    tp = lax.axis_size("tp")
    decoded = exchange(decoded.reshape(tp, groups // tp, -1), "tp")
    decoded = jnp.sum(decoded, axis=0).astype(jnp.bfloat16)

    keys = jnp.where(first_core, mine, theirs)
    values = jnp.where(first_core, theirs, mine)
    kv_cache = jnp.stack([keys, values], axis=1).reshape(slot_dev, block_rows, 2, local_width)
    return (kv_cache, decoded)


def solution(mesh):
    groups, tp = mesh.devices.shape
    fine = Mesh(
        mesh.devices.reshape(Z_CHIPS, X_CHIPS, groups // (Z_CHIPS * X_CHIPS), tp), GROUP + ("tp",)
    )
    placed = (
        P(GROUP, None, None),
        P(GROUP),
        P(),
        P(),
        P(GROUP, None, "tp"),
        P("tp", GROUP),
        P(GROUP, "tp"),
        P(GROUP, None, "tp"),
        P(GROUP),
    )
    return jax.shard_map(
        per_device,
        mesh=fine,
        in_specs=placed,
        out_specs=(P(GROUP, None, None, "tp"), P("tp", GROUP)),
        check_vma=False,
    )
```

```python
import functools
import math

import jax
import jax.numpy as jnp
from jax import lax
from jax.experimental import pallas as pl
from jax.experimental.pallas import tpu as pltpu
from jax.sharding import Mesh
from jax.sharding import PartitionSpec as P

HEAD_DIM = 128
EPSILON = 1e-05
NEG_FILL = -1e30
GROUP = ("z", "x", "core")
MIB = 1 << 20
Z_CHIPS, X_CHIPS = 8, 4
Z_RING, X_RING = (0, -1, 1, -2, 2, -3, 3, 4), (0, -1, 1, 2)
TOP_PARTS, SUM_PARTS = 3, 2


def normalize(saved_rows, norm_gain):
    as_float = saved_rows.astype(jnp.float32)
    inv_rms = lax.rsqrt(jnp.mean(as_float * as_float, axis=-1, keepdims=True) + EPSILON)
    return (as_float * inv_rms * norm_gain.astype(jnp.float32)).astype(jnp.bfloat16)


def lookup(lookup_table, indices):
    matches = indices[..., None] == jnp.arange(lookup_table.shape[0], dtype=jnp.int32)
    return jnp.sum(jnp.where(matches, lookup_table, 0), axis=-1)


def swap_cores(value):
    return lax.ppermute(value, "core", [(0, 1), (1, 0)])


def around(place_ref, axis, chips, ring):
    sign = 1 - 2 * place_ref[2]
    return [lax.rem(place_ref[axis] + sign * step + chips, chips) for step in ring]


def project_kernel(split, place_ref, own_ref, other_ref, cos_ref, sin_ref, *refs):
    a_refs, b_refs = refs[: len(X_RING)], refs[len(X_RING) : len(X_RING) + len(Z_RING)]
    own_out, other_out, query_out, weight = refs[len(X_RING) + len(Z_RING) :]
    core = place_ref[2]
    rows, depth = own_ref.shape
    width = weight.shape[1]
    half = depth // (2 * Z_CHIPS * X_CHIPS)
    extra = a_refs[0].shape[0] // len(Z_RING) - 2 * half

    def place(piece, at, chip, columns):
        for part, whose in ((0, core), (1, 1 - core)):
            to = pl.multiple_of((2 * chip + whose) * half, 16)
            weight[pl.ds(to, half), columns] = piece[pl.ds(at + part * half, half), :]

    for a_ref, x in zip(a_refs, around(place_ref, 1, X_CHIPS, X_RING)):
        for z in range(Z_CHIPS):
            chip = z * X_CHIPS + x
            at = z * (2 * half + extra)
            place(a_ref, at, chip, pl.ds(0, split))
            tiles = a_ref[pl.ds(at + 2 * half, extra), :].astype(jnp.float32)
            query_out[chip, pl.ds(pl.multiple_of(core * 8, 8), 8), :] = tiles[:8]
            query_out[chip, pl.ds(pl.multiple_of(8 - core * 8, 8), 8), :] = tiles[8:16]
    for b_ref, z in zip(b_refs, around(place_ref, 0, Z_CHIPS, Z_RING)):
        for x in range(X_CHIPS):
            place(b_ref, x * 2 * half, z * X_CHIPS + x, pl.ds(split, width - split))

    chunk = 1024 if depth % 1024 == 0 else depth
    for part, (rows_ref, out) in enumerate(((own_ref, own_out), (other_ref, other_out))):
        span = pl.ds(part * rows, rows)
        total = jnp.zeros((rows, width), jnp.float32)
        for k in range(depth // chunk):
            lanes = pl.ds(k * chunk, chunk)
            total += jnp.dot(
                rows_ref[:, lanes], weight[lanes, :], preferred_element_type=jnp.float32
            )
        cosine, sine = cos_ref[span, :], sin_ref[span, :]
        for head in range(width // HEAD_DIM):
            value = total[:, head * HEAD_DIM : (head + 1) * HEAD_DIM]
            turned = value * cosine + pltpu.roll(value, HEAD_DIM // 2, 1) * sine
            out[:, pl.ds(head * HEAD_DIM, HEAD_DIM)] = turned.astype(out.dtype)


def project(place, own, other, cosine, sine, a_blocks, b_blocks):
    rows, depth = own.shape
    split = a_blocks[0].shape[1]
    width = split + b_blocks[0].shape[1]
    out = jax.ShapeDtypeStruct((rows, width), jnp.bfloat16)
    tiles = jax.ShapeDtypeStruct((Z_CHIPS * X_CHIPS, 16, split), jnp.float32)
    vmem = pl.BlockSpec(memory_space=pltpu.VMEM)
    operands = (own, other, cosine, sine, *a_blocks, *b_blocks)
    return pl.pallas_call(
        functools.partial(project_kernel, split),
        in_specs=[pl.BlockSpec(memory_space=pltpu.SMEM)] + [vmem] * len(operands),
        out_specs=[vmem] * 3,
        out_shape=[out, out, tiles],
        scratch_shapes=[pltpu.VMEM((depth, width), jnp.bfloat16)],
        compiler_params=pltpu.CompilerParams(vmem_limit_bytes=40 * MIB),
        cost_estimate=pl.CostEstimate(
            flops=4 * rows * depth * width,
            bytes_accessed=4 * rows * depth + 2 * depth * width,
            transcendentals=0,
        ),
    )(place, *operands)


def attend_kernel(place_ref, mine_ref, theirs_ref, query_ref, keys_ref, out_ref, tiles):
    has_keys = place_ref[2] == 0
    chips = query_ref.shape[0]
    heads = mine_ref.shape[1] // HEAD_DIM
    key_conv = keys_ref[0:1, :]

    def rows_of(part):
        lanes = pl.ds(part % 2 * HEAD_DIM, HEAD_DIM)
        return jnp.concatenate([query_ref[:, core * 8 + part // 2, lanes] for core in (0, 1)])

    allowed = rows_of(heads)[:, 0:1] == key_conv
    lane = lax.broadcasted_iota(jnp.int32, (2 * chips, HEAD_DIM), 1)
    stats = jnp.zeros(lane.shape, jnp.float32)

    def put(row, value):
        for core in (0, 1):
            tiles[:, core, row, :] = value[core * chips : (core + 1) * chips]

    for head in range(heads):
        lanes = pl.ds(head * HEAD_DIM, HEAD_DIM)
        mine, theirs = mine_ref[:, lanes], theirs_ref[:, lanes]
        keys = jnp.where(has_keys, mine, theirs)
        values = jnp.where(has_keys, theirs, mine)
        scores = lax.dot_general(
            rows_of(head).astype(jnp.bfloat16),
            keys,
            (((1,), (1,)), ((), ())),
            preferred_element_type=jnp.float32,
        )
        scores = jnp.where(allowed, scores * (1.0 / math.sqrt(HEAD_DIM)), NEG_FILL)
        top = jnp.max(scores, axis=-1, keepdims=True)
        weight = jnp.where(allowed, jnp.exp(scores - top), 0.0).astype(jnp.bfloat16)
        total = jnp.sum(weight.astype(jnp.float32), axis=-1, keepdims=True)
        put(head, jnp.dot(weight, values, preferred_element_type=jnp.float32))
        at = head
        for value, parts in ((top, TOP_PARTS), (total, SUM_PARTS)):
            for _ in range(parts):
                rounded = value.astype(jnp.bfloat16).astype(jnp.float32)
                stats = jnp.where(lane == at, rounded, stats)
                value = value - rounded
                at += 8
    put(heads, stats)
    for row in range(heads + 1, 8):
        put(row, jnp.zeros_like(stats))
    out_ref[...] = tiles[...].astype(jnp.bfloat16)


def attend(place, mine, theirs, queries, key_conv):
    shape = (queries.shape[0], 2, 8, HEAD_DIM)
    vmem = pl.BlockSpec(memory_space=pltpu.VMEM)
    return pl.pallas_call(
        attend_kernel,
        in_specs=[pl.BlockSpec(memory_space=pltpu.SMEM)] + [vmem] * 4,
        out_specs=vmem,
        out_shape=jax.ShapeDtypeStruct(shape, jnp.bfloat16),
        scratch_shapes=[pltpu.VMEM(shape, jnp.float32)],
        compiler_params=pltpu.CompilerParams(vmem_limit_bytes=16 * MIB),
    )(place, mine, theirs, queries, key_conv)


def merge_kernel(heads, parts_ref, query_ref, new_ref, out_ref, parts, tile):
    parts[...] = parts_ref[...].astype(jnp.float32)
    stats = parts[:, heads, :]
    tile[...] = jnp.zeros_like(tile)
    for head in range(heads):
        lanes = pl.ds(head * HEAD_DIM, HEAD_DIM)
        query = query_ref[:, lanes].astype(jnp.float32)
        own_key = new_ref[0:1, lanes].astype(jnp.float32)
        own_value = new_ref[1:2, lanes].astype(jnp.float32)
        own = jnp.sum(query * own_key, axis=-1, keepdims=True) * (1.0 / math.sqrt(HEAD_DIM))
        stat = [stats[:, head + 8 * k : head + 8 * k + 1] for k in range(TOP_PARTS + SUM_PARTS)]
        top, total = sum(stat[1:TOP_PARTS], stat[0]), sum(stat[TOP_PARTS + 1 :], stat[TOP_PARTS])
        best = jnp.maximum(jnp.max(top, axis=0, keepdims=True), own)
        factor = jnp.exp(top - best)
        own_weight = jnp.exp(own - best).astype(jnp.bfloat16).astype(jnp.float32)
        total = jnp.sum(total * factor, axis=0, keepdims=True) + own_weight
        mixed = jnp.sum(parts[:, head, :] * factor, axis=0, keepdims=True)
        tile[head : head + 1, :] = (mixed + own_weight * own_value) / total
    out_ref[...] = jnp.broadcast_to(tile[...].astype(jnp.bfloat16), out_ref.shape)


def merge(parts, query, new_pair):
    vmem = pl.BlockSpec(memory_space=pltpu.VMEM)
    return pl.pallas_call(
        functools.partial(merge_kernel, query.shape[1] // HEAD_DIM),
        in_specs=[vmem] * 3,
        out_specs=vmem,
        out_shape=jax.ShapeDtypeStruct(parts.shape, jnp.bfloat16),
        scratch_shapes=[
            pltpu.VMEM(parts.shape, jnp.float32),
            pltpu.VMEM(parts.shape[1:], jnp.float32),
        ],
        compiler_params=pltpu.CompilerParams(vmem_limit_bytes=16 * MIB),
    )(parts, query, new_pair)


def send(value, dz, dx):
    pairs = []
    for z in range(Z_CHIPS):
        for x in range(X_CHIPS):
            for core, sign in ((0, 1), (1, -1)):
                to = ((z + sign * dz) % Z_CHIPS * X_CHIPS + (x + sign * dx) % X_CHIPS) * 2 + core
                pairs.append(((z * X_CHIPS + x) * 2 + core, to))
    return lax.ppermute(value, GROUP, pairs)


def ring(value, chips, dz, dx):
    behind, ahead, found = value, value, [value]
    for _ in range(chips // 2 - 1):
        behind, ahead = send(behind, dz, dx), send(ahead, -dz, -dx)
        found += [behind, ahead]
    return found + [send(behind, dz, dx)]


def exchange(value, axis):
    return lax.all_to_all(value, axis, 0, 0, tiled=True)


def collect(piece, axis, chips):
    copies = jnp.broadcast_to(piece, (chips,) + piece.shape)
    return exchange(copies, axis).reshape(chips * piece.shape[0], piece.shape[1])


def per_device(
    saved, block_per_slot, lengths, norm_gain, kv_weight, out_weight, queries, new_kv, row_conv
):
    slot_dev, block_rows, model_width = saved.shape
    groups = lax.axis_size(GROUP)
    blocks_conv = slot_dev * groups // lengths.shape[0]
    local_width = kv_weight.shape[2]
    heads = local_width // HEAD_DIM
    core = lax.axis_index("core")
    first_core = core == 0

    split = 2 * HEAD_DIM
    keep = jnp.where(first_core, kv_weight[:, 0], kv_weight[:, 1])
    give = jnp.where(first_core, kv_weight[:, 1], kv_weight[:, 0])
    numbers = jnp.broadcast_to(row_conv, (HEAD_DIM,)), jnp.pad(block_per_slot, (0, split - slot_dev))
    conv_part, block_part = (part.astype(jnp.bfloat16)[None] for part in numbers)
    wide = jnp.concatenate([queries, conv_part], axis=1)
    rows = [wide[:, at : at + split] for at in range(0, wide.shape[1], split)] + [block_part]
    notes = jnp.pad(jnp.concatenate(rows), ((0, 8 - len(rows)), (0, 0)))
    sent = jnp.concatenate([give, jnp.pad(notes, ((0, 8), (0, local_width - split)))])
    got = swap_cores(sent)
    part_rows = keep.shape[0]
    got_notes = got[part_rows : part_rows + 8, :split]
    piece_a = jnp.concatenate([keep[:, :split], got[:part_rows, :split], notes, got_notes])
    piece_b = jnp.concatenate([keep[:, split:], got[:part_rows, split:]])
    block_b = collect(piece_b, "x", X_CHIPS)
    block_a = collect(piece_a, "z", Z_CHIPS)
    saved, block_b = lax.optimization_barrier((saved, block_b))
    b_blocks = ring(block_b, Z_CHIPS, 1, 0)
    a_blocks = ring(block_a, X_CHIPS, 0, 1)

    normed = normalize(saved, norm_gain).reshape(slot_dev * block_rows, model_width)
    other_normed = swap_cores(normed)
    other_blocks = got_notes[len(rows) - 1, :slot_dev]
    blocks = jnp.concatenate([block_per_slot, other_blocks.astype(jnp.int32)])
    conv = blocks // blocks_conv
    positions = (blocks % blocks_conv * block_rows)[:, None] + jnp.arange(
        block_rows, dtype=jnp.int32
    )
    live = (positions < lookup(lengths, conv)[:, None]).reshape(-1, 1)
    half_dim = HEAD_DIM // 2
    freq_index = jnp.arange(half_dim, dtype=jnp.float32)
    inverse = jnp.exp(freq_index * (-2.0 * math.log(10000.0) / HEAD_DIM))
    angles = positions.reshape(-1, 1).astype(jnp.float32) * inverse
    cosine, sine = jnp.cos(angles), jnp.sin(angles)
    cosine = jnp.where(first_core, jnp.concatenate([cosine, cosine], axis=-1), 1.0)
    sine = jnp.where(first_core, jnp.concatenate([-sine, sine], axis=-1), 0.0)
    cosine, sine = jnp.where(live, cosine, 0.0), jnp.where(live, sine, 0.0)
    own_rows = slot_dev * block_rows
    key_conv = jnp.where(live[:own_rows, 0], jnp.repeat(conv[:slot_dev], block_rows), -1)
    key_conv = jnp.broadcast_to(key_conv.astype(jnp.float32), (8, own_rows))
    place = jnp.stack([lax.axis_index("z"), lax.axis_index("x"), core]).astype(jnp.int32)

    mine, for_other, tiles = project(
        place, normed, other_normed, cosine, sine, a_blocks, b_blocks
    )
    theirs = swap_cores(for_other)
    parts = attend(place, mine, theirs, tiles, key_conv).reshape(groups, 8, HEAD_DIM)
    merged = merge(exchange(parts, GROUP), queries, new_kv[0])
    attended = exchange(merged, GROUP)[:, :heads].reshape(groups, local_width)
    decoded = jnp.dot(attended, out_weight, preferred_element_type=jnp.float32)
    tp = lax.axis_size("tp")
    decoded = exchange(decoded.reshape(tp, groups // tp, -1), "tp")
    decoded = jnp.sum(decoded, axis=0).astype(jnp.bfloat16)

    keys = jnp.where(first_core, mine, theirs)
    values = jnp.where(first_core, theirs, mine)
    kv_cache = jnp.stack([keys, values], axis=1).reshape(slot_dev, block_rows, 2, local_width)
    return (kv_cache, decoded)


def solution(mesh):
    groups, tp = mesh.devices.shape
    fine = Mesh(
        mesh.devices.reshape(Z_CHIPS, X_CHIPS, groups // (Z_CHIPS * X_CHIPS), tp), GROUP + ("tp",)
    )
    placed = (
        P(GROUP, None, None),
        P(GROUP),
        P(),
        P(),
        P(GROUP, None, "tp"),
        P("tp", GROUP),
        P(GROUP, "tp"),
        P(GROUP, None, "tp"),
        P(GROUP),
    )
    return jax.shard_map(
        per_device,
        mesh=fine,
        in_specs=placed,
        out_specs=(P(GROUP, None, None, "tp"), P("tp", GROUP)),
        check_vma=False,
    )
```

```python
import functools
import math

import jax
import jax.numpy as jnp
from jax import lax
from jax.experimental import pallas as pl
from jax.experimental.pallas import tpu as pltpu
from jax.sharding import Mesh
from jax.sharding import PartitionSpec as P

HEAD_DIM = 128
EPSILON = 1e-05
NEG_FILL = -1e30
GROUP = ("z", "x", "core")
MIB = 1 << 20
Z_CHIPS, X_CHIPS = 8, 4
Z_RING, X_RING = (0, -1, 1, -2, 2, -3, 3, 4), (0, -1, 1, 2)
TOP_PARTS, SUM_PARTS = 3, 2


def normalize(saved_rows, norm_gain):
    as_float = saved_rows.astype(jnp.float32)
    inv_rms = lax.rsqrt(jnp.mean(as_float * as_float, axis=-1, keepdims=True) + EPSILON)
    return (as_float * inv_rms * norm_gain.astype(jnp.float32)).astype(jnp.bfloat16)


def lookup(lookup_table, indices):
    matches = indices[..., None] == jnp.arange(lookup_table.shape[0], dtype=jnp.int32)
    return jnp.sum(jnp.where(matches, lookup_table, 0), axis=-1)


def swap_cores(value):
    return lax.ppermute(value, "core", [(0, 1), (1, 0)])


def around(place_ref, axis, chips, ring):
    sign = 1 - 2 * place_ref[2]
    return [lax.rem(place_ref[axis] + sign * step + chips, chips) for step in ring]


def project_rows(core, half, place_pieces, refs):
    own_ref, other_ref, cos_ref, sin_ref, own_out, other_out, weight = refs
    rows, depth = own_ref.shape
    width = weight.shape[1]

    for chip, ref, at in place_pieces:
        for part, whose in ((0, core), (1, 1 - core)):
            to = pl.multiple_of((2 * chip + whose) * half, 16)
            weight[pl.ds(to, half), :] = ref[pl.ds(at + part * half, half), :]

    chunk = 1024 if depth % 1024 == 0 else depth
    for part, (rows_ref, out) in enumerate(((own_ref, own_out), (other_ref, other_out))):
        span = pl.ds(part * rows, rows)
        total = jnp.zeros((rows, width), jnp.float32)
        for k in range(depth // chunk):
            lanes = pl.ds(k * chunk, chunk)
            total += jnp.dot(
                rows_ref[:, lanes], weight[lanes, :], preferred_element_type=jnp.float32
            )
        cosine, sine = cos_ref[span, :], sin_ref[span, :]
        for head in range(width // HEAD_DIM):
            value = total[:, head * HEAD_DIM : (head + 1) * HEAD_DIM]
            turned = value * cosine + pltpu.roll(value, HEAD_DIM // 2, 1) * sine
            out[:, pl.ds(head * HEAD_DIM, HEAD_DIM)] = turned.astype(out.dtype)


def project_a_kernel(place_ref, *refs):
    rows_refs, a_refs = refs[:4], refs[4 : 4 + len(X_RING)]
    own_out, other_out, query_out, weight = refs[4 + len(X_RING) :]
    core = place_ref[2]
    half = weight.shape[0] // (2 * Z_CHIPS * X_CHIPS)
    each = a_refs[0].shape[0] // Z_CHIPS
    pieces = []
    for ref, x in zip(a_refs, around(place_ref, 1, X_CHIPS, X_RING)):
        for z in range(Z_CHIPS):
            chip = z * X_CHIPS + x
            pieces.append((chip, ref, z * each))
            notes = ref[pl.ds(z * each + 2 * half, each - 2 * half), :].astype(jnp.float32)
            query_out[chip, pl.ds(pl.multiple_of(core * 8, 8), 8), :] = notes[:8]
            query_out[chip, pl.ds(pl.multiple_of(8 - core * 8, 8), 8), :] = notes[8:16]
    project_rows(core, half, pieces, (*rows_refs, own_out, other_out, weight))


def project_b_kernel(place_ref, *refs):
    rows_refs, b_refs = refs[:4], refs[4 : 4 + len(Z_RING)]
    own_out, other_out, weight = refs[4 + len(Z_RING) :]
    half = weight.shape[0] // (2 * Z_CHIPS * X_CHIPS)
    pieces = []
    for ref, z in zip(b_refs, around(place_ref, 0, Z_CHIPS, Z_RING)):
        for i, x in enumerate(around(place_ref, 1, X_CHIPS, X_RING)):
            pieces.append((z * X_CHIPS + x, ref, i * 2 * half))
    project_rows(place_ref[2], half, pieces, (*rows_refs, own_out, other_out, weight))


def project(kernel, place, rows, tables, blocks, extra_out=()):
    count, depth = rows[0].shape
    width = blocks[0].shape[1]
    out = jax.ShapeDtypeStruct((count, width), jnp.bfloat16)
    vmem = pl.BlockSpec(memory_space=pltpu.VMEM)
    operands = (*rows, *tables, *blocks)
    return pl.pallas_call(
        kernel,
        in_specs=[pl.BlockSpec(memory_space=pltpu.SMEM)] + [vmem] * len(operands),
        out_specs=[vmem] * (2 + len(extra_out)),
        out_shape=[out, out, *extra_out],
        scratch_shapes=[pltpu.VMEM((depth, width), jnp.bfloat16)],
        compiler_params=pltpu.CompilerParams(vmem_limit_bytes=32 * MIB),
        cost_estimate=pl.CostEstimate(
            flops=4 * count * depth * width,
            bytes_accessed=4 * count * depth + 2 * depth * width,
            transcendentals=0,
        ),
    )(place, *operands)


def attend_kernel(place_ref, mine_a, theirs_a, mine_b, theirs_b, query_ref, keys_ref, out_ref, tiles):
    has_keys = place_ref[2] == 0
    chips = query_ref.shape[0]
    halves = [
        (mine, theirs, head * HEAD_DIM)
        for mine, theirs in ((mine_a, theirs_a), (mine_b, theirs_b))
        for head in range(mine.shape[1] // HEAD_DIM)
    ]
    heads = len(halves)
    key_conv = keys_ref[0:1, :]

    def rows_of(part):
        lanes = pl.ds(part % 2 * HEAD_DIM, HEAD_DIM)
        return jnp.concatenate([query_ref[:, core * 8 + part // 2, lanes] for core in (0, 1)])

    allowed = rows_of(heads)[:, 0:1] == key_conv
    lane = lax.broadcasted_iota(jnp.int32, (2 * chips, HEAD_DIM), 1)
    stats = jnp.zeros(lane.shape, jnp.float32)

    def put(row, value):
        for core in (0, 1):
            tiles[:, core, row, :] = value[core * chips : (core + 1) * chips]

    for head, (mine_ref, theirs_ref, first) in enumerate(halves):
        lanes = pl.ds(first, HEAD_DIM)
        mine, theirs = mine_ref[:, lanes], theirs_ref[:, lanes]
        keys = jnp.where(has_keys, mine, theirs)
        values = jnp.where(has_keys, theirs, mine)
        scores = lax.dot_general(
            rows_of(head).astype(jnp.bfloat16),
            keys,
            (((1,), (1,)), ((), ())),
            preferred_element_type=jnp.float32,
        )
        scores = jnp.where(allowed, scores * (1.0 / math.sqrt(HEAD_DIM)), NEG_FILL)
        top = jnp.max(scores, axis=-1, keepdims=True)
        weight = jnp.where(allowed, jnp.exp(scores - top), 0.0).astype(jnp.bfloat16)
        total = jnp.sum(weight.astype(jnp.float32), axis=-1, keepdims=True)
        put(head, jnp.dot(weight, values, preferred_element_type=jnp.float32))
        at = head
        for value, parts in ((top, TOP_PARTS), (total, SUM_PARTS)):
            for _ in range(parts):
                rounded = value.astype(jnp.bfloat16).astype(jnp.float32)
                stats = jnp.where(lane == at, rounded, stats)
                value = value - rounded
                at += 8
    put(heads, stats)
    for row in range(heads + 1, 8):
        put(row, jnp.zeros_like(stats))
    out_ref[...] = tiles[...].astype(jnp.bfloat16)


def attend(place, halves, queries, key_conv):
    shape = (queries.shape[0], 2, 8, HEAD_DIM)
    vmem = pl.BlockSpec(memory_space=pltpu.VMEM)
    return pl.pallas_call(
        attend_kernel,
        in_specs=[pl.BlockSpec(memory_space=pltpu.SMEM)] + [vmem] * 6,
        out_specs=vmem,
        out_shape=jax.ShapeDtypeStruct(shape, jnp.bfloat16),
        scratch_shapes=[pltpu.VMEM(shape, jnp.float32)],
        compiler_params=pltpu.CompilerParams(vmem_limit_bytes=16 * MIB),
    )(place, *halves, queries, key_conv)


def merge_kernel(heads, parts_ref, query_ref, new_ref, out_ref, parts, tile):
    parts[...] = parts_ref[...].astype(jnp.float32)
    stats = parts[:, heads, :]
    tile[...] = jnp.zeros_like(tile)
    for head in range(heads):
        lanes = pl.ds(head * HEAD_DIM, HEAD_DIM)
        query = query_ref[:, lanes].astype(jnp.float32)
        own_key = new_ref[0:1, lanes].astype(jnp.float32)
        own_value = new_ref[1:2, lanes].astype(jnp.float32)
        own = jnp.sum(query * own_key, axis=-1, keepdims=True) * (1.0 / math.sqrt(HEAD_DIM))
        stat = [stats[:, head + 8 * k : head + 8 * k + 1] for k in range(TOP_PARTS + SUM_PARTS)]
        top, total = sum(stat[1:TOP_PARTS], stat[0]), sum(stat[TOP_PARTS + 1 :], stat[TOP_PARTS])
        best = jnp.maximum(jnp.max(top, axis=0, keepdims=True), own)
        factor = jnp.exp(top - best)
        own_weight = jnp.exp(own - best).astype(jnp.bfloat16).astype(jnp.float32)
        total = jnp.sum(total * factor, axis=0, keepdims=True) + own_weight
        mixed = jnp.sum(parts[:, head, :] * factor, axis=0, keepdims=True)
        tile[head : head + 1, :] = (mixed + own_weight * own_value) / total
    out_ref[...] = jnp.broadcast_to(tile[...].astype(jnp.bfloat16), out_ref.shape)


def merge(parts, query, new_pair):
    vmem = pl.BlockSpec(memory_space=pltpu.VMEM)
    return pl.pallas_call(
        functools.partial(merge_kernel, query.shape[1] // HEAD_DIM),
        in_specs=[vmem] * 3,
        out_specs=vmem,
        out_shape=jax.ShapeDtypeStruct(parts.shape, jnp.bfloat16),
        scratch_shapes=[
            pltpu.VMEM(parts.shape, jnp.float32),
            pltpu.VMEM(parts.shape[1:], jnp.float32),
        ],
        compiler_params=pltpu.CompilerParams(vmem_limit_bytes=16 * MIB),
    )(parts, query, new_pair)


def send(value, dz, dx):
    pairs = []
    for z in range(Z_CHIPS):
        for x in range(X_CHIPS):
            for core, sign in ((0, 1), (1, -1)):
                to = ((z + sign * dz) % Z_CHIPS * X_CHIPS + (x + sign * dx) % X_CHIPS) * 2 + core
                pairs.append(((z * X_CHIPS + x) * 2 + core, to))
    return lax.ppermute(value, GROUP, pairs)


def ring(value, chips, dz, dx):
    behind, ahead, found = value, value, [value]
    for _ in range(chips // 2 - 1):
        behind, ahead = send(behind, dz, dx), send(ahead, -dz, -dx)
        found += [behind, ahead]
    return found + [send(behind, dz, dx)]


def exchange(value, axis):
    return lax.all_to_all(value, axis, 0, 0, tiled=True)


def per_device(
    saved, block_per_slot, lengths, norm_gain, kv_weight, out_weight, queries, new_kv, row_conv
):
    slot_dev, block_rows, model_width = saved.shape
    groups = lax.axis_size(GROUP)
    blocks_conv = slot_dev * groups // lengths.shape[0]
    local_width = kv_weight.shape[2]
    heads = local_width // HEAD_DIM
    core = lax.axis_index("core")
    first_core = core == 0

    split = 2 * HEAD_DIM
    keep = jnp.where(first_core, kv_weight[:, 0], kv_weight[:, 1])
    give = jnp.where(first_core, kv_weight[:, 1], kv_weight[:, 0])
    numbers = jnp.broadcast_to(row_conv, (HEAD_DIM,)), jnp.pad(block_per_slot, (0, split - slot_dev))
    conv_part, block_part = (part.astype(jnp.bfloat16)[None] for part in numbers)
    wide = jnp.concatenate([queries, conv_part], axis=1)
    lines = [wide[:, at : at + split] for at in range(0, wide.shape[1], split)] + [block_part]
    notes = jnp.pad(jnp.concatenate(lines), ((0, 8 - len(lines)), (0, 0)))
    sent = jnp.concatenate([give, jnp.pad(notes, ((0, 8), (0, local_width - split)))])
    got = swap_cores(sent)
    part_rows = keep.shape[0]
    got_notes = got[part_rows : part_rows + 8, :split]
    piece_a = jnp.concatenate([keep[:, :split], got[:part_rows, :split], notes, got_notes])
    piece_b = jnp.concatenate([keep[:, split:], got[:part_rows, split:]])
    copies_a = jnp.broadcast_to(piece_a, (Z_CHIPS,) + piece_a.shape)
    copies_a, piece_b = lax.optimization_barrier((copies_a, piece_b))
    block_a = exchange(copies_a, "z").reshape(Z_CHIPS * piece_a.shape[0], split)
    block_b = jnp.concatenate(
        [piece_b, send(piece_b, 0, 1), send(piece_b, 0, -1), send(piece_b, 0, 2)]
    )
    b_blocks = ring(block_b, Z_CHIPS, 1, 0)
    a_blocks = ring(block_a, X_CHIPS, 0, 1)
    saved, b_blocks[1] = lax.optimization_barrier((saved, b_blocks[1]))

    normed = normalize(saved, norm_gain).reshape(slot_dev * block_rows, model_width)
    other_normed = swap_cores(normed)
    other_blocks = got_notes[len(lines) - 1, :slot_dev]
    blocks = jnp.concatenate([block_per_slot, other_blocks.astype(jnp.int32)])
    conv = blocks // blocks_conv
    positions = (blocks % blocks_conv * block_rows)[:, None] + jnp.arange(
        block_rows, dtype=jnp.int32
    )
    live = (positions < lookup(lengths, conv)[:, None]).reshape(-1, 1)
    half_dim = HEAD_DIM // 2
    freq_index = jnp.arange(half_dim, dtype=jnp.float32)
    inverse = jnp.exp(freq_index * (-2.0 * math.log(10000.0) / HEAD_DIM))
    angles = positions.reshape(-1, 1).astype(jnp.float32) * inverse
    cosine, sine = jnp.cos(angles), jnp.sin(angles)
    cosine = jnp.where(first_core, jnp.concatenate([cosine, cosine], axis=-1), 1.0)
    sine = jnp.where(first_core, jnp.concatenate([-sine, sine], axis=-1), 0.0)
    cosine, sine = jnp.where(live, cosine, 0.0), jnp.where(live, sine, 0.0)
    own_rows = slot_dev * block_rows
    key_conv = jnp.where(live[:own_rows, 0], jnp.repeat(conv[:slot_dev], block_rows), -1)
    key_conv = jnp.broadcast_to(key_conv.astype(jnp.float32), (8, own_rows))
    place = jnp.stack([lax.axis_index("z"), lax.axis_index("x"), core]).astype(jnp.int32)

    rows, tables = (normed, other_normed), (cosine, sine)
    tiles = jax.ShapeDtypeStruct((Z_CHIPS * X_CHIPS, 16, split), jnp.float32)
    mine_a, give_a, tiles = project(project_a_kernel, place, rows, tables, a_blocks, (tiles,))
    theirs_a = swap_cores(give_a)
    mine_b, give_b = project(project_b_kernel, place, rows, tables, b_blocks)
    theirs_b = swap_cores(give_b)
    halves = (mine_a, theirs_a, mine_b, theirs_b)
    parts = attend(place, halves, tiles, key_conv).reshape(groups, 8, HEAD_DIM)
    merged = merge(exchange(parts, GROUP), queries, new_kv[0])
    attended = exchange(merged, GROUP)[:, :heads].reshape(groups, local_width)
    decoded = jnp.dot(attended, out_weight, preferred_element_type=jnp.float32)
    tp = lax.axis_size("tp")
    decoded = exchange(decoded.reshape(tp, groups // tp, -1), "tp")
    decoded = jnp.sum(decoded, axis=0).astype(jnp.bfloat16)

    mine = jnp.concatenate([mine_a, mine_b], axis=1)
    theirs = jnp.concatenate([theirs_a, theirs_b], axis=1)
    keys = jnp.where(first_core, mine, theirs)
    values = jnp.where(first_core, theirs, mine)
    kv_cache = jnp.stack([keys, values], axis=1).reshape(slot_dev, block_rows, 2, local_width)
    return (kv_cache, decoded)


def solution(mesh):
    groups, tp = mesh.devices.shape
    fine = Mesh(
        mesh.devices.reshape(Z_CHIPS, X_CHIPS, groups // (Z_CHIPS * X_CHIPS), tp), GROUP + ("tp",)
    )
    placed = (
        P(GROUP, None, None),
        P(GROUP),
        P(),
        P(),
        P(GROUP, None, "tp"),
        P("tp", GROUP),
        P(GROUP, "tp"),
        P(GROUP, None, "tp"),
        P(GROUP),
    )
    return jax.shard_map(
        per_device,
        mesh=fine,
        in_specs=placed,
        out_specs=(P(GROUP, None, None, "tp"), P("tp", GROUP)),
        check_vma=False,
    )
```

```python
import functools
import math

import jax
import jax.numpy as jnp
from jax import lax
from jax.experimental import pallas as pl
from jax.experimental.pallas import tpu as pltpu
from jax.sharding import Mesh
from jax.sharding import PartitionSpec as P

HEAD_DIM = 128
EPSILON = 1e-05
NEG_FILL = -1e30
GROUP = ("z", "x", "core")
MIB = 1 << 20
Z_CHIPS, X_CHIPS = 8, 4
TOP_PARTS, SUM_PARTS = 3, 2


def normalize(saved_rows, norm_gain):
    as_float = saved_rows.astype(jnp.float32)
    inv_rms = lax.rsqrt(jnp.mean(as_float * as_float, axis=-1, keepdims=True) + EPSILON)
    return (as_float * inv_rms * norm_gain.astype(jnp.float32)).astype(jnp.bfloat16)


def lookup(lookup_table, indices):
    matches = indices[..., None] == jnp.arange(lookup_table.shape[0], dtype=jnp.int32)
    return jnp.sum(jnp.where(matches, lookup_table, 0), axis=-1)


def swap_cores(value):
    return lax.ppermute(value, "core", [(0, 1), (1, 0)])


def around(place_ref, axis, chips, ring):
    sign = 1 - 2 * place_ref[2]
    return [lax.rem(place_ref[axis] + sign * step + chips, chips) for step in ring]


def a_kernel(place_ref, own_ref, other_ref, a_ref, total_out, query_out, weight):
    rows, depth = own_ref.shape
    chips = query_out.shape[0]
    span, each = depth // chips, a_ref.shape[0] // chips
    for chip in range(chips):
        at = chip * each
        weight[pl.ds(chip * span, span), :] = a_ref[pl.ds(at, span), :]
        query_out[chip] = a_ref[pl.ds(at + span, each - span), :].astype(jnp.float32)
    for part, rows_ref in enumerate((own_ref, other_ref)):
        total_out[pl.ds(part * rows, rows), :] = jnp.dot(
            rows_ref[...], weight[...], preferred_element_type=jnp.float32
        )


def b_total(place_ref, steps, rows_ref, blocks):
    total = None
    for block, z in zip(blocks, around(place_ref, 0, Z_CHIPS, steps)):
        features = block.shape[0]
        lanes = pl.ds(pl.multiple_of(z * features, HEAD_DIM), features)
        product = jnp.dot(rows_ref[:, lanes], block[...], preferred_element_type=jnp.float32)
        total = product if total is None else total + product
    return total


def b_kernel(steps, place_ref, own_ref, other_ref, *refs):
    *blocks, total_out = refs
    rows = own_ref.shape[0]
    for part, rows_ref in enumerate((own_ref, other_ref)):
        total_out[pl.ds(part * rows, rows), :] = b_total(place_ref, steps, rows_ref, blocks)


def last_kernel(steps, place_ref, own_ref, other_ref, a_ref, b_ref, cos_ref, sin_ref, *refs):
    *blocks, own_out, other_out = refs
    rows = own_ref.shape[0]
    for part, (rows_ref, out) in enumerate(((own_ref, own_out), (other_ref, other_out))):
        span = pl.ds(part * rows, rows)
        cosine, sine = cos_ref[span, :], sin_ref[span, :]
        rest = b_ref[span, :] + b_total(place_ref, steps, rows_ref, blocks)
        at = 0
        for total in (a_ref[span, :], rest):
            for first in range(0, total.shape[1], HEAD_DIM):
                value = total[:, first : first + HEAD_DIM]
                turned = value * cosine + pltpu.roll(value, HEAD_DIM // 2, 1) * sine
                out[:, pl.ds(at, HEAD_DIM)] = turned.astype(out.dtype)
                at += HEAD_DIM


def project(kernel, place, operands, blocks, out_shape, features, scratch=()):
    vmem = pl.BlockSpec(memory_space=pltpu.VMEM)
    width = blocks[0].shape[1]
    count = 2 * operands[0].shape[0]
    return pl.pallas_call(
        kernel,
        in_specs=[pl.BlockSpec(memory_space=pltpu.SMEM)] + [vmem] * (len(operands) + len(blocks)),
        out_specs=[vmem] * len(out_shape),
        out_shape=out_shape,
        scratch_shapes=scratch,
        compiler_params=pltpu.CompilerParams(vmem_limit_bytes=32 * MIB),
        cost_estimate=pl.CostEstimate(
            flops=2 * count * features * width,
            bytes_accessed=2 * count * features + 2 * features * width,
            transcendentals=0,
        ),
    )(place, *operands, *blocks)


def attend_kernel(place_ref, mine_ref, theirs_ref, query_ref, keys_ref, out_ref, tiles):
    has_keys = place_ref[2] == 0
    chips = query_ref.shape[0]
    heads = mine_ref.shape[1] // HEAD_DIM
    key_conv = keys_ref[0:1, :]

    def rows_of(part):
        lanes = pl.ds(part % 2 * HEAD_DIM, HEAD_DIM)
        return jnp.concatenate([query_ref[:, core * 8 + part // 2, lanes] for core in (0, 1)])

    allowed = rows_of(heads)[:, 0:1] == key_conv
    lane = lax.broadcasted_iota(jnp.int32, (2 * chips, HEAD_DIM), 1)
    stats = jnp.zeros(lane.shape, jnp.float32)

    def put(row, value):
        for core in (0, 1):
            tiles[:, core, row, :] = value[core * chips : (core + 1) * chips]

    for head in range(heads):
        lanes = pl.ds(head * HEAD_DIM, HEAD_DIM)
        mine, theirs = mine_ref[:, lanes], theirs_ref[:, lanes]
        keys = jnp.where(has_keys, mine, theirs)
        values = jnp.where(has_keys, theirs, mine)
        scores = lax.dot_general(
            rows_of(head).astype(jnp.bfloat16),
            keys,
            (((1,), (1,)), ((), ())),
            preferred_element_type=jnp.float32,
        )
        scores = jnp.where(allowed, scores * (1.0 / math.sqrt(HEAD_DIM)), NEG_FILL)
        top = jnp.max(scores, axis=-1, keepdims=True)
        weight = jnp.where(allowed, jnp.exp(scores - top), 0.0).astype(jnp.bfloat16)
        total = jnp.sum(weight.astype(jnp.float32), axis=-1, keepdims=True)
        put(head, jnp.dot(weight, values, preferred_element_type=jnp.float32))
        at = head
        for value, parts in ((top, TOP_PARTS), (total, SUM_PARTS)):
            for _ in range(parts):
                rounded = value.astype(jnp.bfloat16).astype(jnp.float32)
                stats = jnp.where(lane == at, rounded, stats)
                value = value - rounded
                at += 8
    put(heads, stats)
    for row in range(heads + 1, 8):
        put(row, jnp.zeros_like(stats))
    out_ref[...] = tiles[...].astype(jnp.bfloat16)


def attend(place, mine, theirs, queries, key_conv):
    shape = (queries.shape[0], 2, 8, HEAD_DIM)
    vmem = pl.BlockSpec(memory_space=pltpu.VMEM)
    return pl.pallas_call(
        attend_kernel,
        in_specs=[pl.BlockSpec(memory_space=pltpu.SMEM)] + [vmem] * 4,
        out_specs=vmem,
        out_shape=jax.ShapeDtypeStruct(shape, jnp.bfloat16),
        scratch_shapes=[pltpu.VMEM(shape, jnp.float32)],
        compiler_params=pltpu.CompilerParams(vmem_limit_bytes=16 * MIB),
    )(place, mine, theirs, queries, key_conv)


def merge_kernel(heads, parts_ref, query_ref, new_ref, out_ref, parts, tile):
    parts[...] = parts_ref[...].astype(jnp.float32)
    stats = parts[:, heads, :]
    tile[...] = jnp.zeros_like(tile)
    for head in range(heads):
        lanes = pl.ds(head * HEAD_DIM, HEAD_DIM)
        query = query_ref[:, lanes].astype(jnp.float32)
        own_key = new_ref[0:1, lanes].astype(jnp.float32)
        own_value = new_ref[1:2, lanes].astype(jnp.float32)
        own = jnp.sum(query * own_key, axis=-1, keepdims=True) * (1.0 / math.sqrt(HEAD_DIM))
        stat = [stats[:, head + 8 * k : head + 8 * k + 1] for k in range(TOP_PARTS + SUM_PARTS)]
        top, total = sum(stat[1:TOP_PARTS], stat[0]), sum(stat[TOP_PARTS + 1 :], stat[TOP_PARTS])
        best = jnp.maximum(jnp.max(top, axis=0, keepdims=True), own)
        factor = jnp.exp(top - best)
        own_weight = jnp.exp(own - best).astype(jnp.bfloat16).astype(jnp.float32)
        total = jnp.sum(total * factor, axis=0, keepdims=True) + own_weight
        mixed = jnp.sum(parts[:, head, :] * factor, axis=0, keepdims=True)
        tile[head : head + 1, :] = (mixed + own_weight * own_value) / total
    out_ref[...] = jnp.broadcast_to(tile[...].astype(jnp.bfloat16), out_ref.shape)


def merge(parts, query, new_pair):
    vmem = pl.BlockSpec(memory_space=pltpu.VMEM)
    return pl.pallas_call(
        functools.partial(merge_kernel, query.shape[1] // HEAD_DIM),
        in_specs=[vmem] * 3,
        out_specs=vmem,
        out_shape=jax.ShapeDtypeStruct(parts.shape, jnp.bfloat16),
        scratch_shapes=[
            pltpu.VMEM(parts.shape, jnp.float32),
            pltpu.VMEM(parts.shape[1:], jnp.float32),
        ],
        compiler_params=pltpu.CompilerParams(vmem_limit_bytes=16 * MIB),
    )(parts, query, new_pair)


def send(value, step):
    pairs = []
    for z in range(Z_CHIPS):
        for x in range(X_CHIPS):
            for core, sign in ((0, 1), (1, -1)):
                to = ((z + sign * step) % Z_CHIPS * X_CHIPS + x) * 2 + core
                pairs.append(((z * X_CHIPS + x) * 2 + core, to))
    return lax.ppermute(value, GROUP, pairs)


def exchange(value, axis):
    return lax.all_to_all(value, axis, 0, 0, tiled=True)


def per_device(
    saved, block_per_slot, lengths, norm_gain, kv_weight, out_weight, queries, new_kv, row_conv
):
    slot_dev, block_rows, model_width = saved.shape
    groups = lax.axis_size(GROUP)
    blocks_conv = slot_dev * groups // lengths.shape[0]
    local_width = kv_weight.shape[2]
    heads = local_width // HEAD_DIM
    core = lax.axis_index("core")
    first_core = core == 0

    split = 2 * HEAD_DIM
    given = jnp.stack([kv_weight[:, kind, split:] for kind in (0, 1)])
    given = jnp.broadcast_to(given, (X_CHIPS,) + given.shape)
    block_b = exchange(given.reshape(-1, *given.shape[2:]), ("x", "core"))
    block_b = block_b.reshape(-1, local_width - split)
    keep = jnp.where(first_core, kv_weight[:, 0, :split], kv_weight[:, 1, :split])
    give = jnp.where(first_core, kv_weight[:, 1, :split], kv_weight[:, 0, :split])
    part_rows = keep.shape[0]
    numbers = jnp.concatenate([row_conv, block_per_slot]).astype(jnp.bfloat16)
    numbers = jnp.broadcast_to(numbers[:, None], (1 + slot_dev, split))
    wide = jnp.concatenate([queries, numbers[:1, :HEAD_DIM]], axis=1)
    lines = [wide[:, at : at + split] for at in range(0, wide.shape[1], split)]
    notes = jnp.concatenate([*lines, numbers[1:]])
    notes = jnp.pad(notes, ((0, 8 - notes.shape[0]), (0, 0)))
    sent = jnp.concatenate([give, jnp.pad(notes, ((0, 8), (0, 0)))])
    got = swap_cores(sent)
    got_notes = got[part_rows : part_rows + 8]
    got = got[:part_rows]
    first = jnp.where(first_core, keep, got), jnp.where(first_core, notes, got_notes)
    second = jnp.where(first_core, got, keep), jnp.where(first_core, got_notes, notes)
    piece_a = jnp.concatenate([first[0], second[0], first[1], second[1]])
    all_a = lax.all_gather(piece_a, ("z", "x"), axis=0, tiled=True)
    saved, block_b = lax.optimization_barrier((saved, block_b))
    behind1, ahead1 = send(block_b, 1), send(block_b, -1)
    behind2, ahead2 = send(behind1, 1), send(ahead1, -1)
    behind3, ahead3 = send(behind2, 1), send(ahead2, -1)

    normed = normalize(saved, norm_gain).reshape(slot_dev * block_rows, model_width)
    other_normed = swap_cores(normed)
    other_blocks = got_notes[len(lines) : len(lines) + slot_dev, 0]
    blocks = jnp.concatenate([block_per_slot, other_blocks.astype(jnp.int32)])
    conv = blocks // blocks_conv
    positions = (blocks % blocks_conv * block_rows)[:, None] + jnp.arange(
        block_rows, dtype=jnp.int32
    )
    live = (positions < lookup(lengths, conv)[:, None]).reshape(-1, 1)
    half_dim = HEAD_DIM // 2
    freq_index = jnp.arange(half_dim, dtype=jnp.float32)
    inverse = jnp.exp(freq_index * (-2.0 * math.log(10000.0) / HEAD_DIM))
    angles = positions.reshape(-1, 1).astype(jnp.float32) * inverse
    cosine, sine = jnp.cos(angles), jnp.sin(angles)
    cosine = jnp.where(first_core, jnp.concatenate([cosine, cosine], axis=-1), 1.0)
    sine = jnp.where(first_core, jnp.concatenate([-sine, sine], axis=-1), 0.0)
    cosine, sine = jnp.where(live, cosine, 0.0), jnp.where(live, sine, 0.0)
    own_rows = slot_dev * block_rows
    key_conv = jnp.where(live[:own_rows, 0], jnp.repeat(conv[:slot_dev], block_rows), -1)
    key_conv = jnp.broadcast_to(key_conv.astype(jnp.float32), (8, own_rows))
    place = jnp.stack([lax.axis_index("z"), lax.axis_index("x"), core]).astype(jnp.int32)

    rows, count = (normed, other_normed), 2 * own_rows
    shapes = [(count, local_width - split), (count, split), (Z_CHIPS * X_CHIPS, 16, split)]
    b_out, a_out, query_out = (jax.ShapeDtypeStruct(shape, jnp.float32) for shape in shapes)
    early, late = (0, -1, 1, -2, 2), (-3, 3, 4)
    features = model_width // Z_CHIPS
    blocks = (block_b, behind1, ahead1, behind2, ahead2)
    (b_part,) = project(
        functools.partial(b_kernel, early), place, rows, blocks, [b_out], len(early) * features
    )
    behind3, b_part = lax.optimization_barrier((behind3, b_part))
    weight = pltpu.VMEM((model_width, split), jnp.bfloat16)
    outs = [a_out, query_out]
    a_part, tiles = project(a_kernel, place, rows, (all_a,), outs, model_width, (weight,))
    blocks = (behind3, ahead3, send(behind3, 1))
    out = jax.ShapeDtypeStruct((own_rows, local_width), jnp.bfloat16)
    mine, give = project(
        functools.partial(last_kernel, late),
        place,
        (*rows, a_part, b_part, cosine, sine),
        blocks,
        [out, out],
        len(late) * features,
    )
    theirs = swap_cores(give)
    parts = attend(place, mine, theirs, tiles, key_conv).reshape(groups, 8, HEAD_DIM)
    merged = merge(exchange(parts, GROUP), queries, new_kv[0])
    attended = exchange(merged, GROUP)[:, :heads].reshape(groups, local_width)
    decoded = jnp.dot(attended, out_weight, preferred_element_type=jnp.float32)
    tp = lax.axis_size("tp")
    decoded = exchange(decoded.reshape(tp, groups // tp, -1), "tp")
    decoded = jnp.sum(decoded, axis=0).astype(jnp.bfloat16)

    keys = jnp.where(first_core, mine, theirs)
    values = jnp.where(first_core, theirs, mine)
    kv_cache = jnp.stack([keys, values], axis=1).reshape(slot_dev, block_rows, 2, local_width)
    return (kv_cache, decoded)


def solution(mesh):
    groups, tp = mesh.devices.shape
    fine = Mesh(
        mesh.devices.reshape(Z_CHIPS, X_CHIPS, groups // (Z_CHIPS * X_CHIPS), tp), GROUP + ("tp",)
    )
    placed = (
        P(GROUP, None, None),
        P(GROUP),
        P(),
        P(),
        P(GROUP, None, "tp"),
        P("tp", GROUP),
        P(GROUP, "tp"),
        P(GROUP, None, "tp"),
        P(GROUP),
    )
    return jax.shard_map(
        per_device,
        mesh=fine,
        in_specs=placed,
        out_specs=(P(GROUP, None, None, "tp"), P("tp", GROUP)),
        check_vma=False,
    )
```

```python
import functools
import math

import jax
import jax.numpy as jnp
from jax import lax
from jax.experimental import pallas as pl
from jax.experimental.pallas import tpu as pltpu
from jax.sharding import Mesh
from jax.sharding import PartitionSpec as P

HEAD_DIM = 128
EPSILON = 1e-05
NEG_FILL = -1e30
GROUP = ("z", "x", "core")
MIB = 1 << 20
Z_CHIPS, X_CHIPS = 8, 4
X_RING = (0, -1, 1, 2)
TOP_PARTS, SUM_PARTS = 3, 2


def normalize(saved_rows, norm_gain):
    as_float = saved_rows.astype(jnp.float32)
    inv_rms = lax.rsqrt(jnp.mean(as_float * as_float, axis=-1, keepdims=True) + EPSILON)
    return (as_float * inv_rms * norm_gain.astype(jnp.float32)).astype(jnp.bfloat16)


def lookup(lookup_table, indices):
    matches = indices[..., None] == jnp.arange(lookup_table.shape[0], dtype=jnp.int32)
    return jnp.sum(jnp.where(matches, lookup_table, 0), axis=-1)


def swap_cores(value):
    return lax.ppermute(value, "core", [(0, 1), (1, 0)])


def around(place_ref, axis, chips, ring):
    sign = 1 - 2 * place_ref[2]
    return [lax.rem(place_ref[axis] + sign * step + chips, chips) for step in ring]


def a_kernel(place_ref, own_ref, other_ref, *refs):
    a_refs = refs[: len(X_RING)]
    total_out, query_out, weight = refs[len(X_RING) :]
    rows, depth = own_ref.shape
    span = depth // (Z_CHIPS * X_CHIPS)
    each = a_refs[0].shape[0] // Z_CHIPS
    for ref, x in zip(a_refs, around(place_ref, 1, X_CHIPS, X_RING)):
        for z in range(Z_CHIPS):
            chip = z * X_CHIPS + x
            weight[pl.ds(pl.multiple_of(chip * span, 16), span), :] = ref[pl.ds(z * each, span), :]
            notes = ref[pl.ds(z * each + span, each - span), :]
            query_out[chip] = notes.astype(jnp.float32)
    for part, rows_ref in enumerate((own_ref, other_ref)):
        total_out[pl.ds(part * rows, rows), :] = jnp.dot(
            rows_ref[...], weight[...], preferred_element_type=jnp.float32
        )


def b_total(place_ref, steps, rows_ref, blocks):
    total = None
    for block, z in zip(blocks, around(place_ref, 0, Z_CHIPS, steps)):
        features = block.shape[0]
        lanes = pl.ds(pl.multiple_of(z * features, HEAD_DIM), features)
        product = jnp.dot(rows_ref[:, lanes], block[...], preferred_element_type=jnp.float32)
        total = product if total is None else total + product
    return total


def b_kernel(steps, place_ref, own_ref, other_ref, *refs):
    *blocks, total_out = refs
    rows = own_ref.shape[0]
    for part, rows_ref in enumerate((own_ref, other_ref)):
        total_out[pl.ds(part * rows, rows), :] = b_total(place_ref, steps, rows_ref, blocks)


def last_kernel(steps, place_ref, own_ref, other_ref, a_ref, b_ref, cos_ref, sin_ref, *refs):
    *blocks, own_out, other_out = refs
    rows = own_ref.shape[0]
    for part, (rows_ref, out) in enumerate(((own_ref, own_out), (other_ref, other_out))):
        span = pl.ds(part * rows, rows)
        cosine, sine = cos_ref[span, :], sin_ref[span, :]
        rest = b_ref[span, :] + b_total(place_ref, steps, rows_ref, blocks)
        at = 0
        for total in (a_ref[span, :], rest):
            for first in range(0, total.shape[1], HEAD_DIM):
                value = total[:, first : first + HEAD_DIM]
                turned = value * cosine + pltpu.roll(value, HEAD_DIM // 2, 1) * sine
                out[:, pl.ds(at, HEAD_DIM)] = turned.astype(out.dtype)
                at += HEAD_DIM


def project(kernel, place, operands, blocks, out_shape, features, scratch=()):
    vmem = pl.BlockSpec(memory_space=pltpu.VMEM)
    width = blocks[0].shape[1]
    count = 2 * operands[0].shape[0]
    return pl.pallas_call(
        kernel,
        in_specs=[pl.BlockSpec(memory_space=pltpu.SMEM)] + [vmem] * (len(operands) + len(blocks)),
        out_specs=[vmem] * len(out_shape),
        out_shape=out_shape,
        scratch_shapes=scratch,
        compiler_params=pltpu.CompilerParams(vmem_limit_bytes=32 * MIB),
        cost_estimate=pl.CostEstimate(
            flops=2 * count * features * width,
            bytes_accessed=2 * count * features + 2 * features * width,
            transcendentals=0,
        ),
    )(place, *operands, *blocks)


def attend_kernel(place_ref, mine_ref, theirs_ref, query_ref, keys_ref, out_ref, tiles):
    has_keys = place_ref[2] == 0
    chips = query_ref.shape[0]
    heads = mine_ref.shape[1] // HEAD_DIM
    key_conv = keys_ref[0:1, :]

    def rows_of(part):
        lanes = pl.ds(part % 2 * HEAD_DIM, HEAD_DIM)
        return jnp.concatenate([query_ref[:, core * 8 + part // 2, lanes] for core in (0, 1)])

    allowed = rows_of(heads)[:, 0:1] == key_conv
    lane = lax.broadcasted_iota(jnp.int32, (2 * chips, HEAD_DIM), 1)
    stats = jnp.zeros(lane.shape, jnp.float32)

    def put(row, value):
        for core in (0, 1):
            tiles[:, core, row, :] = value[core * chips : (core + 1) * chips]

    for head in range(heads):
        lanes = pl.ds(head * HEAD_DIM, HEAD_DIM)
        mine, theirs = mine_ref[:, lanes], theirs_ref[:, lanes]
        keys = jnp.where(has_keys, mine, theirs)
        values = jnp.where(has_keys, theirs, mine)
        scores = lax.dot_general(
            rows_of(head).astype(jnp.bfloat16),
            keys,
            (((1,), (1,)), ((), ())),
            preferred_element_type=jnp.float32,
        )
        scores = jnp.where(allowed, scores * (1.0 / math.sqrt(HEAD_DIM)), NEG_FILL)
        top = jnp.max(scores, axis=-1, keepdims=True)
        weight = jnp.where(allowed, jnp.exp(scores - top), 0.0).astype(jnp.bfloat16)
        total = jnp.sum(weight.astype(jnp.float32), axis=-1, keepdims=True)
        put(head, jnp.dot(weight, values, preferred_element_type=jnp.float32))
        at = head
        for value, parts in ((top, TOP_PARTS), (total, SUM_PARTS)):
            for _ in range(parts):
                rounded = value.astype(jnp.bfloat16).astype(jnp.float32)
                stats = jnp.where(lane == at, rounded, stats)
                value = value - rounded
                at += 8
    put(heads, stats)
    for row in range(heads + 1, 8):
        put(row, jnp.zeros_like(stats))
    out_ref[...] = tiles[...].astype(jnp.bfloat16)


def attend(place, mine, theirs, queries, key_conv):
    shape = (queries.shape[0], 2, 8, HEAD_DIM)
    vmem = pl.BlockSpec(memory_space=pltpu.VMEM)
    return pl.pallas_call(
        attend_kernel,
        in_specs=[pl.BlockSpec(memory_space=pltpu.SMEM)] + [vmem] * 4,
        out_specs=vmem,
        out_shape=jax.ShapeDtypeStruct(shape, jnp.bfloat16),
        scratch_shapes=[pltpu.VMEM(shape, jnp.float32)],
        compiler_params=pltpu.CompilerParams(vmem_limit_bytes=16 * MIB),
    )(place, mine, theirs, queries, key_conv)


def merge_kernel(heads, parts_ref, query_ref, new_ref, out_ref, parts, tile):
    parts[...] = parts_ref[...].astype(jnp.float32)
    stats = parts[:, heads, :]
    tile[...] = jnp.zeros_like(tile)
    for head in range(heads):
        lanes = pl.ds(head * HEAD_DIM, HEAD_DIM)
        query = query_ref[:, lanes].astype(jnp.float32)
        own_key = new_ref[0:1, lanes].astype(jnp.float32)
        own_value = new_ref[1:2, lanes].astype(jnp.float32)
        own = jnp.sum(query * own_key, axis=-1, keepdims=True) * (1.0 / math.sqrt(HEAD_DIM))
        stat = [stats[:, head + 8 * k : head + 8 * k + 1] for k in range(TOP_PARTS + SUM_PARTS)]
        top, total = sum(stat[1:TOP_PARTS], stat[0]), sum(stat[TOP_PARTS + 1 :], stat[TOP_PARTS])
        best = jnp.maximum(jnp.max(top, axis=0, keepdims=True), own)
        factor = jnp.exp(top - best)
        own_weight = jnp.exp(own - best).astype(jnp.bfloat16).astype(jnp.float32)
        total = jnp.sum(total * factor, axis=0, keepdims=True) + own_weight
        mixed = jnp.sum(parts[:, head, :] * factor, axis=0, keepdims=True)
        tile[head : head + 1, :] = (mixed + own_weight * own_value) / total
    out_ref[...] = jnp.broadcast_to(tile[...].astype(jnp.bfloat16), out_ref.shape)


def merge(parts, query, new_pair):
    vmem = pl.BlockSpec(memory_space=pltpu.VMEM)
    return pl.pallas_call(
        functools.partial(merge_kernel, query.shape[1] // HEAD_DIM),
        in_specs=[vmem] * 3,
        out_specs=vmem,
        out_shape=jax.ShapeDtypeStruct(parts.shape, jnp.bfloat16),
        scratch_shapes=[
            pltpu.VMEM(parts.shape, jnp.float32),
            pltpu.VMEM(parts.shape[1:], jnp.float32),
        ],
        compiler_params=pltpu.CompilerParams(vmem_limit_bytes=16 * MIB),
    )(parts, query, new_pair)


def send(value, dz, dx):
    pairs = []
    for z in range(Z_CHIPS):
        for x in range(X_CHIPS):
            for core, sign in ((0, 1), (1, -1)):
                to = ((z + sign * dz) % Z_CHIPS * X_CHIPS + (x + sign * dx) % X_CHIPS) * 2 + core
                pairs.append(((z * X_CHIPS + x) * 2 + core, to))
    return lax.ppermute(value, GROUP, pairs)


def exchange(value, axis):
    return lax.all_to_all(value, axis, 0, 0, tiled=True)


def per_device(
    saved, block_per_slot, lengths, norm_gain, kv_weight, out_weight, queries, new_kv, row_conv
):
    slot_dev, block_rows, model_width = saved.shape
    groups = lax.axis_size(GROUP)
    blocks_conv = slot_dev * groups // lengths.shape[0]
    local_width = kv_weight.shape[2]
    heads = local_width // HEAD_DIM
    core = lax.axis_index("core")
    first_core = core == 0

    split = 2 * HEAD_DIM
    given = jnp.stack([kv_weight[:, kind, split:] for kind in (0, 1)])
    given = jnp.broadcast_to(given, (X_CHIPS,) + given.shape)
    given, kv_weight, a_queries = lax.optimization_barrier((given, kv_weight, queries))
    block_b = exchange(given.reshape(-1, *given.shape[2:]), ("x", "core"))
    block_b = block_b.reshape(-1, local_width - split)
    keep = jnp.where(first_core, kv_weight[:, 0, :split], kv_weight[:, 1, :split])
    give = jnp.where(first_core, kv_weight[:, 1, :split], kv_weight[:, 0, :split])
    part_rows = keep.shape[0]
    numbers = jnp.concatenate([row_conv, block_per_slot]).astype(jnp.bfloat16)
    numbers = jnp.broadcast_to(numbers[:, None], (1 + slot_dev, split))
    wide = jnp.concatenate([a_queries, numbers[:1, :HEAD_DIM]], axis=1)
    lines = [wide[:, at : at + split] for at in range(0, wide.shape[1], split)]
    notes = jnp.concatenate([*lines, numbers[1:]])
    notes = jnp.pad(notes, ((0, 8 - notes.shape[0]), (0, 0)))
    sent = jnp.concatenate([give, jnp.pad(notes, ((0, 8), (0, 0)))])
    got = swap_cores(sent)
    got_notes = got[part_rows : part_rows + 8]
    got = got[:part_rows]
    first = jnp.where(first_core, keep, got), jnp.where(first_core, notes, got_notes)
    second = jnp.where(first_core, got, keep), jnp.where(first_core, got_notes, notes)
    piece_a = jnp.concatenate([first[0], second[0], first[1], second[1]])
    copies_a = jnp.broadcast_to(piece_a, (Z_CHIPS,) + piece_a.shape)
    saved, block_b, copies_a = lax.optimization_barrier((saved, block_b, copies_a))
    block_a = exchange(copies_a, "z").reshape(-1, split)
    a_behind, a_ahead = send(block_a, 0, 1), send(block_a, 0, -1)
    a_blocks = (block_a, a_behind, a_ahead, send(a_behind, 0, 1))
    behind1, ahead1 = send(block_b, 1, 0), send(block_b, -1, 0)
    behind2, ahead2 = send(behind1, 1, 0), send(ahead1, -1, 0)
    behind3, ahead3 = send(behind2, 1, 0), send(ahead2, -1, 0)

    normed = normalize(saved, norm_gain).reshape(slot_dev * block_rows, model_width)
    other_normed = swap_cores(normed)
    other_blocks = got_notes[len(lines) : len(lines) + slot_dev, 0]
    blocks = jnp.concatenate([block_per_slot, other_blocks.astype(jnp.int32)])
    conv = blocks // blocks_conv
    positions = (blocks % blocks_conv * block_rows)[:, None] + jnp.arange(
        block_rows, dtype=jnp.int32
    )
    live = (positions < lookup(lengths, conv)[:, None]).reshape(-1, 1)
    half_dim = HEAD_DIM // 2
    freq_index = jnp.arange(half_dim, dtype=jnp.float32)
    inverse = jnp.exp(freq_index * (-2.0 * math.log(10000.0) / HEAD_DIM))
    angles = positions.reshape(-1, 1).astype(jnp.float32) * inverse
    cosine, sine = jnp.cos(angles), jnp.sin(angles)
    cosine = jnp.where(first_core, jnp.concatenate([cosine, cosine], axis=-1), 1.0)
    sine = jnp.where(first_core, jnp.concatenate([-sine, sine], axis=-1), 0.0)
    cosine, sine = jnp.where(live, cosine, 0.0), jnp.where(live, sine, 0.0)
    own_rows = slot_dev * block_rows
    key_conv = jnp.where(live[:own_rows, 0], jnp.repeat(conv[:slot_dev], block_rows), -1)
    key_conv = jnp.broadcast_to(key_conv.astype(jnp.float32), (8, own_rows))
    place = jnp.stack([lax.axis_index("z"), lax.axis_index("x"), core]).astype(jnp.int32)

    rows, count = (normed, other_normed), 2 * own_rows
    shapes = [(count, local_width - split), (count, split), (Z_CHIPS * X_CHIPS, 16, split)]
    b_out, a_out, query_out = (jax.ShapeDtypeStruct(shape, jnp.float32) for shape in shapes)
    early, late = (0, -1, 1, -2, 2), (-3, 3, 4)
    features = model_width // Z_CHIPS
    blocks = (block_b, behind1, ahead1, behind2, ahead2)
    (b_part,) = project(
        functools.partial(b_kernel, early), place, rows, blocks, [b_out], len(early) * features
    )
    behind3, b_part = lax.optimization_barrier((behind3, b_part))
    weight = pltpu.VMEM((model_width, split), jnp.bfloat16)
    outs = [a_out, query_out]
    a_part, tiles = project(a_kernel, place, rows, a_blocks, outs, model_width, (weight,))
    blocks = (behind3, ahead3, send(behind3, 1, 0))
    out = jax.ShapeDtypeStruct((own_rows, local_width), jnp.bfloat16)
    mine, give = project(
        functools.partial(last_kernel, late),
        place,
        (*rows, a_part, b_part, cosine, sine),
        blocks,
        [out, out],
        len(late) * features,
    )
    theirs = swap_cores(give)
    parts = attend(place, mine, theirs, tiles, key_conv).reshape(groups, 8, HEAD_DIM)
    merged = merge(exchange(parts, GROUP), queries, new_kv[0])
    attended = exchange(merged, GROUP)[:, :heads].reshape(groups, local_width)
    decoded = jnp.dot(attended, out_weight, preferred_element_type=jnp.float32)
    tp = lax.axis_size("tp")
    decoded = exchange(decoded.reshape(tp, groups // tp, -1), "tp")
    decoded = jnp.sum(decoded, axis=0).astype(jnp.bfloat16)

    keys = jnp.where(first_core, mine, theirs)
    values = jnp.where(first_core, theirs, mine)
    kv_cache = jnp.stack([keys, values], axis=1).reshape(slot_dev, block_rows, 2, local_width)
    return (kv_cache, decoded)


def solution(mesh):
    groups, tp = mesh.devices.shape
    fine = Mesh(
        mesh.devices.reshape(Z_CHIPS, X_CHIPS, groups // (Z_CHIPS * X_CHIPS), tp), GROUP + ("tp",)
    )
    placed = (
        P(GROUP, None, None),
        P(GROUP),
        P(),
        P(),
        P(GROUP, None, "tp"),
        P("tp", GROUP),
        P(GROUP, "tp"),
        P(GROUP, None, "tp"),
        P(GROUP),
    )
    return jax.shard_map(
        per_device,
        mesh=fine,
        in_specs=placed,
        out_specs=(P(GROUP, None, None, "tp"), P("tp", GROUP)),
        check_vma=False,
    )
```

```python
import functools
import math

import jax
import jax.numpy as jnp
from jax import lax
from jax.experimental import pallas as pl
from jax.experimental.pallas import tpu as pltpu
from jax.sharding import Mesh
from jax.sharding import PartitionSpec as P

HEAD_DIM = 128
EPSILON = 1e-05
NEG_FILL = -1e30
GROUP = ("z", "x", "core")
MIB = 1 << 20
Z_CHIPS, X_CHIPS = 8, 4
Z_RING, X_RING = (0, -1, 1, -2, 2, -3, 3, 4), (0, -1, 1, 2)
TOP_PARTS, SUM_PARTS = 3, 2


def normalize(saved_rows, norm_gain):
    as_float = saved_rows.astype(jnp.float32)
    inv_rms = lax.rsqrt(jnp.mean(as_float * as_float, axis=-1, keepdims=True) + EPSILON)
    return (as_float * inv_rms * norm_gain.astype(jnp.float32)).astype(jnp.bfloat16)


def lookup(lookup_table, indices):
    matches = indices[..., None] == jnp.arange(lookup_table.shape[0], dtype=jnp.int32)
    return jnp.sum(jnp.where(matches, lookup_table, 0), axis=-1)


def swap_cores(value):
    return lax.ppermute(value, "core", [(0, 1), (1, 0)])


def around(place_ref, axis, chips, ring):
    sign = 1 - 2 * place_ref[2]
    return [lax.rem(place_ref[axis] + sign * step + chips, chips) for step in ring]


def project_kernel(place_ref, own_ref, other_ref, cos_ref, sin_ref, *refs):
    a_refs, b_refs = refs[: len(X_RING)], refs[len(X_RING) : len(X_RING) + len(Z_RING)]
    own_out, other_out, query_out, weight = refs[len(X_RING) + len(Z_RING) :]
    rows, depth = own_ref.shape
    width = weight.shape[1]
    devices, split = query_out.shape[0], query_out.shape[2]
    span, features = depth // devices, b_refs[0].shape[0]

    for ref, x in zip(a_refs, around(place_ref, 1, X_CHIPS, X_RING)):
        for z in range(Z_CHIPS):
            for core in (0, 1):
                device = (z * X_CHIPS + x) * 2 + core
                to = pl.ds(pl.multiple_of(device * span, 16), span)
                piece = ref[2 * z + core]
                weight[to, pl.ds(0, split)] = piece[:span]
                query_out[device] = piece[span:].astype(jnp.float32)
    for ref, z in zip(b_refs, around(place_ref, 0, Z_CHIPS, Z_RING)):
        to = pl.ds(pl.multiple_of(z * features, 16), features)
        weight[to, pl.ds(split, width - split)] = ref[...]

    chunk = 1024 if depth % 1024 == 0 else depth
    for part, (rows_ref, out) in enumerate(((own_ref, own_out), (other_ref, other_out))):
        span = pl.ds(part * rows, rows)
        total = jnp.zeros((rows, width), jnp.float32)
        for k in range(depth // chunk):
            lanes = pl.ds(k * chunk, chunk)
            total += jnp.dot(
                rows_ref[:, lanes], weight[lanes, :], preferred_element_type=jnp.float32
            )
        cosine, sine = cos_ref[span, :], sin_ref[span, :]
        for head in range(width // HEAD_DIM):
            value = total[:, head * HEAD_DIM : (head + 1) * HEAD_DIM]
            turned = value * cosine + pltpu.roll(value, HEAD_DIM // 2, 1) * sine
            out[:, pl.ds(head * HEAD_DIM, HEAD_DIM)] = turned.astype(out.dtype)


def project(place, own, other, cosine, sine, a_blocks, b_blocks):
    rows, depth = own.shape
    split = a_blocks[0].shape[2]
    width = split + b_blocks[0].shape[1]
    lines = a_blocks[0].shape[1] - depth // (2 * Z_CHIPS * X_CHIPS)
    out = jax.ShapeDtypeStruct((rows, width), jnp.bfloat16)
    notes = jax.ShapeDtypeStruct((2 * Z_CHIPS * X_CHIPS, lines, split), jnp.float32)
    vmem = pl.BlockSpec(memory_space=pltpu.VMEM)
    operands = (own, other, cosine, sine, *a_blocks, *b_blocks)
    return pl.pallas_call(
        project_kernel,
        in_specs=[pl.BlockSpec(memory_space=pltpu.SMEM)] + [vmem] * len(operands),
        out_specs=[vmem] * 3,
        out_shape=[out, out, notes],
        scratch_shapes=[pltpu.VMEM((depth, width), jnp.bfloat16)],
        compiler_params=pltpu.CompilerParams(vmem_limit_bytes=40 * MIB),
        cost_estimate=pl.CostEstimate(
            flops=4 * rows * depth * width,
            bytes_accessed=4 * rows * depth + 2 * depth * width,
            transcendentals=0,
        ),
    )(place, *operands)


def attend_kernel(place_ref, mine_ref, theirs_ref, query_ref, keys_ref, out_ref, tiles):
    has_keys = place_ref[2] == 0
    count = query_ref.shape[0]
    heads = mine_ref.shape[1] // HEAD_DIM
    key_conv = keys_ref[0:1, :]

    def rows_of(part):
        return query_ref[:, part // 2, pl.ds(part % 2 * HEAD_DIM, HEAD_DIM)]

    allowed = rows_of(heads)[:, 0:1] == key_conv
    lane = lax.broadcasted_iota(jnp.int32, (count, HEAD_DIM), 1)
    stats = jnp.zeros(lane.shape, jnp.float32)
    for head in range(heads):
        lanes = pl.ds(head * HEAD_DIM, HEAD_DIM)
        mine, theirs = mine_ref[:, lanes], theirs_ref[:, lanes]
        keys = jnp.where(has_keys, mine, theirs)
        values = jnp.where(has_keys, theirs, mine)
        scores = lax.dot_general(
            rows_of(head).astype(jnp.bfloat16),
            keys,
            (((1,), (1,)), ((), ())),
            preferred_element_type=jnp.float32,
        )
        scores = jnp.where(allowed, scores * (1.0 / math.sqrt(HEAD_DIM)), NEG_FILL)
        top = jnp.max(scores, axis=-1, keepdims=True)
        weight = jnp.where(allowed, jnp.exp(scores - top), 0.0).astype(jnp.bfloat16)
        total = jnp.sum(weight.astype(jnp.float32), axis=-1, keepdims=True)
        tiles[:, head, :] = jnp.dot(weight, values, preferred_element_type=jnp.float32)
        at = head
        for value, parts in ((top, TOP_PARTS), (total, SUM_PARTS)):
            for _ in range(parts):
                rounded = value.astype(jnp.bfloat16).astype(jnp.float32)
                stats = jnp.where(lane == at, rounded, stats)
                value = value - rounded
                at += 8
    tiles[:, heads, :] = stats
    for row in range(heads + 1, 8):
        tiles[:, row, :] = jnp.zeros_like(stats)
    out_ref[...] = tiles[...].astype(jnp.bfloat16)


def attend(place, mine, theirs, queries, key_conv):
    shape = (queries.shape[0], 8, HEAD_DIM)
    vmem = pl.BlockSpec(memory_space=pltpu.VMEM)
    return pl.pallas_call(
        attend_kernel,
        in_specs=[pl.BlockSpec(memory_space=pltpu.SMEM)] + [vmem] * 4,
        out_specs=vmem,
        out_shape=jax.ShapeDtypeStruct(shape, jnp.bfloat16),
        scratch_shapes=[pltpu.VMEM(shape, jnp.float32)],
        compiler_params=pltpu.CompilerParams(vmem_limit_bytes=16 * MIB),
    )(place, mine, theirs, queries, key_conv)


def merge_kernel(heads, parts_ref, query_ref, new_ref, out_ref, parts, tile):
    parts[...] = parts_ref[...].astype(jnp.float32)
    stats = parts[:, heads, :]
    tile[...] = jnp.zeros_like(tile)
    for head in range(heads):
        lanes = pl.ds(head * HEAD_DIM, HEAD_DIM)
        query = query_ref[:, lanes].astype(jnp.float32)
        own_key = new_ref[0:1, lanes].astype(jnp.float32)
        own_value = new_ref[1:2, lanes].astype(jnp.float32)
        own = jnp.sum(query * own_key, axis=-1, keepdims=True) * (1.0 / math.sqrt(HEAD_DIM))
        stat = [stats[:, head + 8 * k : head + 8 * k + 1] for k in range(TOP_PARTS + SUM_PARTS)]
        top, total = sum(stat[1:TOP_PARTS], stat[0]), sum(stat[TOP_PARTS + 1 :], stat[TOP_PARTS])
        best = jnp.maximum(jnp.max(top, axis=0, keepdims=True), own)
        factor = jnp.exp(top - best)
        own_weight = jnp.exp(own - best).astype(jnp.bfloat16).astype(jnp.float32)
        total = jnp.sum(total * factor, axis=0, keepdims=True) + own_weight
        mixed = jnp.sum(parts[:, head, :] * factor, axis=0, keepdims=True)
        tile[head : head + 1, :] = (mixed + own_weight * own_value) / total
    out_ref[...] = jnp.broadcast_to(tile[...].astype(jnp.bfloat16), out_ref.shape)


def merge(parts, query, new_pair):
    vmem = pl.BlockSpec(memory_space=pltpu.VMEM)
    return pl.pallas_call(
        functools.partial(merge_kernel, query.shape[1] // HEAD_DIM),
        in_specs=[vmem] * 3,
        out_specs=vmem,
        out_shape=jax.ShapeDtypeStruct(parts.shape, jnp.bfloat16),
        scratch_shapes=[
            pltpu.VMEM(parts.shape, jnp.float32),
            pltpu.VMEM(parts.shape[1:], jnp.float32),
        ],
        compiler_params=pltpu.CompilerParams(vmem_limit_bytes=16 * MIB),
    )(parts, query, new_pair)


def send(value, dz, dx):
    pairs = []
    for z in range(Z_CHIPS):
        for x in range(X_CHIPS):
            for core, sign in ((0, 1), (1, -1)):
                to = ((z + sign * dz) % Z_CHIPS * X_CHIPS + (x + sign * dx) % X_CHIPS) * 2 + core
                pairs.append(((z * X_CHIPS + x) * 2 + core, to))
    return lax.ppermute(value, GROUP, pairs)


def exchange(value, axis):
    return lax.all_to_all(value, axis, 0, 0, tiled=True)


def per_device(
    saved, block_per_slot, lengths, norm_gain, kv_weight, out_weight, queries, new_kv, row_conv
):
    slot_dev, block_rows, model_width = saved.shape
    groups = lax.axis_size(GROUP)
    blocks_conv = slot_dev * groups // lengths.shape[0]
    local_width = kv_weight.shape[2]
    heads = local_width // HEAD_DIM
    core = lax.axis_index("core")
    first_core = core == 0

    split = 2 * HEAD_DIM
    def copies(pieces, chips):
        pieces = jnp.broadcast_to(jnp.stack(pieces), (chips, 2) + pieces[0].shape)
        return pieces.reshape(-1, *pieces.shape[2:])

    part_rows = kv_weight.shape[0]
    block_b = exchange(copies([kv_weight[:, k, split:] for k in (0, 1)], X_CHIPS), ("x", "core"))
    block_b = block_b.reshape(-1, local_width - split)
    numbers = jnp.concatenate([row_conv, block_per_slot]).astype(jnp.bfloat16)
    numbers = jnp.broadcast_to(numbers[:, None], (1 + slot_dev, split))
    wide = jnp.concatenate([queries, numbers[:1, :HEAD_DIM]], axis=1)
    lines = [wide[:, at : at + split] for at in range(0, wide.shape[1], split)]
    notes = jnp.concatenate([*lines, numbers[1:]])
    notes = jnp.pad(notes, ((0, 8 - notes.shape[0]), (0, 0)))
    pieces_a = [jnp.concatenate([kv_weight[:, k, :split], notes]) for k in (0, 1)]
    copies_a = copies(pieces_a, Z_CHIPS)
    pieces_a = exchange(copies_a, ("z", "core"))
    saved, block_b, _ = lax.optimization_barrier((saved, block_b, copies_a))
    a_behind, a_ahead = send(pieces_a, 0, 1), send(pieces_a, 0, -1)
    behind1, ahead1 = send(block_b, 1, 0), send(block_b, -1, 0)
    ahead1, a_behind = lax.optimization_barrier((ahead1, a_behind))
    behind2, ahead2 = send(behind1, 1, 0), send(ahead1, -1, 0)
    ahead2, a_ahead = lax.optimization_barrier((ahead2, a_ahead))
    behind3, ahead3 = send(behind2, 1, 0), send(ahead2, -1, 0)
    a_blocks = (pieces_a, a_behind, a_ahead, send(a_behind, 0, 1))
    b_blocks = (block_b, behind1, ahead1, behind2, ahead2, behind3, ahead3, send(behind3, 1, 0))

    normed = normalize(saved, norm_gain).reshape(slot_dev * block_rows, model_width)
    other_normed = swap_cores(normed)
    beside = 2 * lax.axis_index("z") + 1 - core
    other_blocks = lax.dynamic_index_in_dim(pieces_a, beside, keepdims=False)
    first_line = part_rows + len(lines)
    other_blocks = other_blocks[first_line : first_line + slot_dev, 0]
    blocks = jnp.concatenate([block_per_slot, other_blocks.astype(jnp.int32)])
    conv = blocks // blocks_conv
    positions = (blocks % blocks_conv * block_rows)[:, None] + jnp.arange(
        block_rows, dtype=jnp.int32
    )
    live = (positions < lookup(lengths, conv)[:, None]).reshape(-1, 1)
    half_dim = HEAD_DIM // 2
    freq_index = jnp.arange(half_dim, dtype=jnp.float32)
    inverse = jnp.exp(freq_index * (-2.0 * math.log(10000.0) / HEAD_DIM))
    angles = positions.reshape(-1, 1).astype(jnp.float32) * inverse
    cosine, sine = jnp.cos(angles), jnp.sin(angles)
    cosine = jnp.where(first_core, jnp.concatenate([cosine, cosine], axis=-1), 1.0)
    sine = jnp.where(first_core, jnp.concatenate([-sine, sine], axis=-1), 0.0)
    cosine, sine = jnp.where(live, cosine, 0.0), jnp.where(live, sine, 0.0)
    own_rows = slot_dev * block_rows
    key_conv = jnp.where(live[:own_rows, 0], jnp.repeat(conv[:slot_dev], block_rows), -1)
    key_conv = jnp.broadcast_to(key_conv.astype(jnp.float32), (8, own_rows))
    place = jnp.stack([lax.axis_index("z"), lax.axis_index("x"), core]).astype(jnp.int32)

    mine, give, tiles = project(
        place, normed, other_normed, cosine, sine, a_blocks, b_blocks
    )
    theirs = swap_cores(give)
    parts = attend(place, mine, theirs, tiles, key_conv)
    merged = merge(exchange(parts, GROUP), queries, new_kv[0])
    attended = exchange(merged, GROUP)[:, :heads].reshape(groups, local_width)
    decoded = jnp.dot(attended, out_weight, preferred_element_type=jnp.float32)
    tp = lax.axis_size("tp")
    decoded = exchange(decoded.reshape(tp, groups // tp, -1), "tp")
    decoded = jnp.sum(decoded, axis=0).astype(jnp.bfloat16)

    keys = jnp.where(first_core, mine, theirs)
    values = jnp.where(first_core, theirs, mine)
    kv_cache = jnp.stack([keys, values], axis=1).reshape(slot_dev, block_rows, 2, local_width)
    return (kv_cache, decoded)


def solution(mesh):
    groups, tp = mesh.devices.shape
    fine = Mesh(
        mesh.devices.reshape(Z_CHIPS, X_CHIPS, groups // (Z_CHIPS * X_CHIPS), tp), GROUP + ("tp",)
    )
    placed = (
        P(GROUP, None, None),
        P(GROUP),
        P(),
        P(),
        P(GROUP, None, "tp"),
        P("tp", GROUP),
        P(GROUP, "tp"),
        P(GROUP, None, "tp"),
        P(GROUP),
    )
    return jax.shard_map(
        per_device,
        mesh=fine,
        in_specs=placed,
        out_specs=(P(GROUP, None, None, "tp"), P("tp", GROUP)),
        check_vma=False,
    )
```

```python
import functools
import math

import jax
import jax.numpy as jnp
from jax import lax
from jax.experimental import pallas as pl
from jax.experimental.pallas import tpu as pltpu
from jax.sharding import Mesh
from jax.sharding import PartitionSpec as P

HEAD_DIM = 128
EPSILON = 1e-05
NEG_FILL = -1e30
GROUP = ("z", "x", "core")
MIB = 1 << 20
Z_CHIPS, X_CHIPS = 8, 4
Z_RING, X_RING = (0, -1, 1, -2, 2, -3, 3, 4), (0, -1, 1, 2)
TOP_PARTS, SUM_PARTS = 3, 2


def normalize(saved_rows, norm_gain):
    as_float = saved_rows.astype(jnp.float32)
    inv_rms = lax.rsqrt(jnp.mean(as_float * as_float, axis=-1, keepdims=True) + EPSILON)
    return (as_float * inv_rms * norm_gain.astype(jnp.float32)).astype(jnp.bfloat16)


def lookup(lookup_table, indices):
    matches = indices[..., None] == jnp.arange(lookup_table.shape[0], dtype=jnp.int32)
    return jnp.sum(jnp.where(matches, lookup_table, 0), axis=-1)


def swap_cores(value):
    return lax.ppermute(value, "core", [(0, 1), (1, 0)])


def around(place_ref, axis, chips, ring):
    sign = 1 - 2 * place_ref[2]
    return [lax.rem(place_ref[axis] + sign * step + chips, chips) for step in ring]


def project_kernel(place_ref, own_ref, other_ref, cos_ref, sin_ref, *refs):
    a_refs, b_refs = refs[: len(X_RING)], refs[len(X_RING) : len(X_RING) + len(Z_RING)]
    own_out, other_out, query_out, weight = refs[len(X_RING) + len(Z_RING) :]
    rows, depth = own_ref.shape
    width = weight.shape[1]
    devices, split = query_out.shape[0], query_out.shape[2]
    span, features = depth // devices, b_refs[0].shape[0]

    for ref, x in zip(a_refs, around(place_ref, 1, X_CHIPS, X_RING)):
        for z in range(Z_CHIPS):
            for core in (0, 1):
                device = (z * X_CHIPS + x) * 2 + core
                to = pl.ds(pl.multiple_of(device * span, 16), span)
                piece = ref[2 * z + core]
                weight[to, pl.ds(0, split)] = piece[:span]
                query_out[device] = piece[span:].astype(jnp.float32)
    for ref, z in zip(b_refs, around(place_ref, 0, Z_CHIPS, Z_RING)):
        to = pl.ds(pl.multiple_of(z * features, 16), features)
        weight[to, pl.ds(split, width - split)] = ref[...]

    chunk = 1024 if depth % 1024 == 0 else depth
    for part, (rows_ref, out) in enumerate(((own_ref, own_out), (other_ref, other_out))):
        span = pl.ds(part * rows, rows)
        total = jnp.zeros((rows, width), jnp.float32)
        for k in range(depth // chunk):
            lanes = pl.ds(k * chunk, chunk)
            total += jnp.dot(
                rows_ref[:, lanes], weight[lanes, :], preferred_element_type=jnp.float32
            )
        cosine, sine = cos_ref[span, :], sin_ref[span, :]
        for head in range(width // HEAD_DIM):
            value = total[:, head * HEAD_DIM : (head + 1) * HEAD_DIM]
            turned = value * cosine + pltpu.roll(value, HEAD_DIM // 2, 1) * sine
            out[:, pl.ds(head * HEAD_DIM, HEAD_DIM)] = turned.astype(out.dtype)


def project(place, own, other, cosine, sine, a_blocks, b_blocks):
    rows, depth = own.shape
    split = a_blocks[0].shape[2]
    width = split + b_blocks[0].shape[1]
    lines = a_blocks[0].shape[1] - depth // (2 * Z_CHIPS * X_CHIPS)
    out = jax.ShapeDtypeStruct((rows, width), jnp.bfloat16)
    notes = jax.ShapeDtypeStruct((2 * Z_CHIPS * X_CHIPS, lines, split), jnp.float32)
    vmem = pl.BlockSpec(memory_space=pltpu.VMEM)
    operands = (own, other, cosine, sine, *a_blocks, *b_blocks)
    return pl.pallas_call(
        project_kernel,
        in_specs=[pl.BlockSpec(memory_space=pltpu.SMEM)] + [vmem] * len(operands),
        out_specs=[vmem] * 3,
        out_shape=[out, out, notes],
        scratch_shapes=[pltpu.VMEM((depth, width), jnp.bfloat16)],
        compiler_params=pltpu.CompilerParams(vmem_limit_bytes=40 * MIB),
        cost_estimate=pl.CostEstimate(
            flops=4 * rows * depth * width,
            bytes_accessed=4 * rows * depth + 2 * depth * width,
            transcendentals=0,
        ),
    )(place, *operands)


def attend_kernel(place_ref, mine_ref, theirs_ref, query_ref, keys_ref, out_ref, tiles):
    has_keys = place_ref[2] == 0
    count = query_ref.shape[0]
    heads = mine_ref.shape[1] // HEAD_DIM
    key_conv = keys_ref[0:1, :]

    def rows_of(part):
        return query_ref[:, part // 2, pl.ds(part % 2 * HEAD_DIM, HEAD_DIM)]

    allowed = rows_of(heads)[:, 0:1] == key_conv
    lane = lax.broadcasted_iota(jnp.int32, (count, HEAD_DIM), 1)
    stats = jnp.zeros(lane.shape, jnp.float32)
    for head in range(heads):
        lanes = pl.ds(head * HEAD_DIM, HEAD_DIM)
        mine, theirs = mine_ref[:, lanes], theirs_ref[:, lanes]
        keys = jnp.where(has_keys, mine, theirs)
        values = jnp.where(has_keys, theirs, mine)
        scores = lax.dot_general(
            rows_of(head).astype(jnp.bfloat16),
            keys,
            (((1,), (1,)), ((), ())),
            preferred_element_type=jnp.float32,
        )
        scores = jnp.where(allowed, scores * (1.0 / math.sqrt(HEAD_DIM)), NEG_FILL)
        top = jnp.max(scores, axis=-1, keepdims=True)
        weight = jnp.where(allowed, jnp.exp(scores - top), 0.0).astype(jnp.bfloat16)
        total = jnp.sum(weight.astype(jnp.float32), axis=-1, keepdims=True)
        tiles[:, head, :] = jnp.dot(weight, values, preferred_element_type=jnp.float32)
        at = head
        for value, parts in ((top, TOP_PARTS), (total, SUM_PARTS)):
            for _ in range(parts):
                rounded = value.astype(jnp.bfloat16).astype(jnp.float32)
                stats = jnp.where(lane == at, rounded, stats)
                value = value - rounded
                at += 8
    tiles[:, heads, :] = stats
    for row in range(heads + 1, 8):
        tiles[:, row, :] = jnp.zeros_like(stats)
    out_ref[...] = tiles[...].astype(jnp.bfloat16)


def attend(place, mine, theirs, queries, key_conv):
    shape = (queries.shape[0], 8, HEAD_DIM)
    vmem = pl.BlockSpec(memory_space=pltpu.VMEM)
    return pl.pallas_call(
        attend_kernel,
        in_specs=[pl.BlockSpec(memory_space=pltpu.SMEM)] + [vmem] * 4,
        out_specs=vmem,
        out_shape=jax.ShapeDtypeStruct(shape, jnp.bfloat16),
        scratch_shapes=[pltpu.VMEM(shape, jnp.float32)],
        compiler_params=pltpu.CompilerParams(vmem_limit_bytes=16 * MIB),
    )(place, mine, theirs, queries, key_conv)


def merge_kernel(heads, parts_ref, query_ref, new_ref, out_ref, parts, tile):
    parts[...] = parts_ref[...].astype(jnp.float32)
    stats = parts[:, heads, :]
    tile[...] = jnp.zeros_like(tile)
    for head in range(heads):
        lanes = pl.ds(head * HEAD_DIM, HEAD_DIM)
        query = query_ref[:, lanes].astype(jnp.float32)
        own_key = new_ref[0:1, lanes].astype(jnp.float32)
        own_value = new_ref[1:2, lanes].astype(jnp.float32)
        own = jnp.sum(query * own_key, axis=-1, keepdims=True) * (1.0 / math.sqrt(HEAD_DIM))
        stat = [stats[:, head + 8 * k : head + 8 * k + 1] for k in range(TOP_PARTS + SUM_PARTS)]
        top, total = sum(stat[1:TOP_PARTS], stat[0]), sum(stat[TOP_PARTS + 1 :], stat[TOP_PARTS])
        best = jnp.maximum(jnp.max(top, axis=0, keepdims=True), own)
        factor = jnp.exp(top - best)
        own_weight = jnp.exp(own - best).astype(jnp.bfloat16).astype(jnp.float32)
        total = jnp.sum(total * factor, axis=0, keepdims=True) + own_weight
        mixed = jnp.sum(parts[:, head, :] * factor, axis=0, keepdims=True)
        tile[head : head + 1, :] = (mixed + own_weight * own_value) / total
    out_ref[...] = jnp.broadcast_to(tile[...].astype(jnp.bfloat16), out_ref.shape)


def merge(parts, query, new_pair):
    vmem = pl.BlockSpec(memory_space=pltpu.VMEM)
    return pl.pallas_call(
        functools.partial(merge_kernel, query.shape[1] // HEAD_DIM),
        in_specs=[vmem] * 3,
        out_specs=vmem,
        out_shape=jax.ShapeDtypeStruct(parts.shape, jnp.bfloat16),
        scratch_shapes=[
            pltpu.VMEM(parts.shape, jnp.float32),
            pltpu.VMEM(parts.shape[1:], jnp.float32),
        ],
        compiler_params=pltpu.CompilerParams(vmem_limit_bytes=16 * MIB),
    )(parts, query, new_pair)


def send(value, dz, dx):
    pairs = []
    for z in range(Z_CHIPS):
        for x in range(X_CHIPS):
            for core, sign in ((0, 1), (1, -1)):
                to = ((z + sign * dz) % Z_CHIPS * X_CHIPS + (x + sign * dx) % X_CHIPS) * 2 + core
                pairs.append(((z * X_CHIPS + x) * 2 + core, to))
    return lax.ppermute(value, GROUP, pairs)


def exchange(value, axis):
    return lax.all_to_all(value, axis, 0, 0, tiled=True)


def per_device(
    saved, block_per_slot, lengths, norm_gain, kv_weight, out_weight, queries, new_kv, row_conv
):
    slot_dev, block_rows, model_width = saved.shape
    groups = lax.axis_size(GROUP)
    blocks_conv = slot_dev * groups // lengths.shape[0]
    local_width = kv_weight.shape[2]
    heads = local_width // HEAD_DIM
    core = lax.axis_index("core")
    first_core = core == 0

    split = 2 * HEAD_DIM
    def copies(pieces, chips):
        pieces = jnp.broadcast_to(jnp.stack(pieces), (chips, 2) + pieces[0].shape)
        return pieces.reshape(-1, *pieces.shape[2:])

    part_rows = kv_weight.shape[0]
    block_b = exchange(copies([kv_weight[:, k, split:] for k in (0, 1)], X_CHIPS), ("x", "core"))
    block_b = block_b.reshape(-1, local_width - split)
    numbers = jnp.concatenate([row_conv, block_per_slot]).astype(jnp.bfloat16)
    numbers = jnp.broadcast_to(numbers[:, None], (1 + slot_dev, split))
    wide = jnp.concatenate([queries, numbers[:1, :HEAD_DIM]], axis=1)
    lines = [wide[:, at : at + split] for at in range(0, wide.shape[1], split)]
    notes = jnp.concatenate([*lines, numbers[1:]])
    notes = jnp.pad(notes, ((0, 8 - notes.shape[0]), (0, 0)))
    pieces_a = [jnp.concatenate([kv_weight[:, k, :split], notes]) for k in (0, 1)]
    copies_a = copies(pieces_a, Z_CHIPS)
    pieces_a = exchange(copies_a, ("z", "core"))
    saved, block_b, _ = lax.optimization_barrier((saved, block_b, copies_a))
    a_behind, a_ahead = send(pieces_a, 0, 1), send(pieces_a, 0, -1)
    behind1, ahead1 = send(block_b, 1, 0), send(block_b, -1, 0)
    behind2, ahead2 = send(behind1, 1, 0), send(ahead1, -1, 0)
    behind3, ahead3 = send(behind2, 1, 0), send(ahead2, -1, 0)
    a_blocks = (pieces_a, a_behind, a_ahead, send(a_behind, 0, 1))
    b_blocks = (block_b, behind1, ahead1, behind2, ahead2, behind3, ahead3, send(behind3, 1, 0))

    normed = normalize(saved, norm_gain).reshape(slot_dev * block_rows, model_width)
    other_normed = swap_cores(normed)
    beside = 2 * lax.axis_index("z") + 1 - core
    other_blocks = lax.dynamic_index_in_dim(pieces_a, beside, keepdims=False)
    first_line = part_rows + len(lines)
    other_blocks = other_blocks[first_line : first_line + slot_dev, 0]
    blocks = jnp.concatenate([block_per_slot, other_blocks.astype(jnp.int32)])
    conv = blocks // blocks_conv
    positions = (blocks % blocks_conv * block_rows)[:, None] + jnp.arange(
        block_rows, dtype=jnp.int32
    )
    live = (positions < lookup(lengths, conv)[:, None]).reshape(-1, 1)
    half_dim = HEAD_DIM // 2
    freq_index = jnp.arange(half_dim, dtype=jnp.float32)
    inverse = jnp.exp(freq_index * (-2.0 * math.log(10000.0) / HEAD_DIM))
    angles = positions.reshape(-1, 1).astype(jnp.float32) * inverse
    cosine, sine = jnp.cos(angles), jnp.sin(angles)
    cosine = jnp.where(first_core, jnp.concatenate([cosine, cosine], axis=-1), 1.0)
    sine = jnp.where(first_core, jnp.concatenate([-sine, sine], axis=-1), 0.0)
    cosine, sine = jnp.where(live, cosine, 0.0), jnp.where(live, sine, 0.0)
    own_rows = slot_dev * block_rows
    key_conv = jnp.where(live[:own_rows, 0], jnp.repeat(conv[:slot_dev], block_rows), -1)
    key_conv = jnp.broadcast_to(key_conv.astype(jnp.float32), (8, own_rows))
    place = jnp.stack([lax.axis_index("z"), lax.axis_index("x"), core]).astype(jnp.int32)

    mine, give, tiles = project(
        place, normed, other_normed, cosine, sine, a_blocks, b_blocks
    )
    theirs = swap_cores(give)
    parts = attend(place, mine, theirs, tiles, key_conv)
    merged = merge(exchange(parts, GROUP), queries, new_kv[0])
    attended = exchange(merged, GROUP)[:, :heads].reshape(groups, local_width)
    decoded = jnp.dot(attended, out_weight, preferred_element_type=jnp.float32)
    tp = lax.axis_size("tp")
    decoded = exchange(decoded.reshape(tp, groups // tp, -1), "tp")
    decoded = jnp.sum(decoded, axis=0).astype(jnp.bfloat16)

    keys = jnp.where(first_core, mine, theirs)
    values = jnp.where(first_core, theirs, mine)
    kv_cache = jnp.stack([keys, values], axis=1).reshape(slot_dev, block_rows, 2, local_width)
    return (kv_cache, decoded)


def solution(mesh):
    groups, tp = mesh.devices.shape
    fine = Mesh(
        mesh.devices.reshape(Z_CHIPS, X_CHIPS, groups // (Z_CHIPS * X_CHIPS), tp), GROUP + ("tp",)
    )
    placed = (
        P(GROUP, None, None),
        P(GROUP),
        P(),
        P(),
        P(GROUP, None, "tp"),
        P("tp", GROUP),
        P(GROUP, "tp"),
        P(GROUP, None, "tp"),
        P(GROUP),
    )
    return jax.shard_map(
        per_device,
        mesh=fine,
        in_specs=placed,
        out_specs=(P(GROUP, None, None, "tp"), P("tp", GROUP)),
        check_vma=False,
    )
```

```python
import functools
import math

import jax
import jax.numpy as jnp
from jax import lax
from jax.experimental import pallas as pl
from jax.experimental.pallas import tpu as pltpu
from jax.sharding import Mesh
from jax.sharding import PartitionSpec as P

HEAD_DIM = 128
EPSILON = 1e-05
NEG_FILL = -1e30
GROUP = ("z", "x", "core")
MIB = 1 << 20
Z_CHIPS, X_CHIPS = 8, 4
Z_RING, X_RING = (0, -1, 1, -2, 2, -3, 3, 4), (0, -1, 1, 2)
TOP_PARTS, SUM_PARTS = 3, 2


def normalize(saved_rows, norm_gain):
    as_float = saved_rows.astype(jnp.float32)
    inv_rms = lax.rsqrt(jnp.mean(as_float * as_float, axis=-1, keepdims=True) + EPSILON)
    return (as_float * inv_rms * norm_gain.astype(jnp.float32)).astype(jnp.bfloat16)


def lookup(lookup_table, indices):
    matches = indices[..., None] == jnp.arange(lookup_table.shape[0], dtype=jnp.int32)
    return jnp.sum(jnp.where(matches, lookup_table, 0), axis=-1)


def swap_cores(value):
    return lax.ppermute(value, "core", [(0, 1), (1, 0)])


def around(place_ref, axis, chips, ring):
    sign = 1 - 2 * place_ref[2]
    return [lax.rem(place_ref[axis] + sign * step + chips, chips) for step in ring]


def project_kernel(place_ref, own_ref, other_ref, cos_ref, sin_ref, *refs):
    a_refs, b_refs = refs[: len(X_RING)], refs[len(X_RING) : len(X_RING) + len(Z_RING)]
    own_out, other_out, query_out, weight = refs[len(X_RING) + len(Z_RING) :]
    rows, depth = own_ref.shape
    width = weight.shape[1]
    devices, split = query_out.shape[0], query_out.shape[2]
    span, features = depth // devices, b_refs[0].shape[0]

    for ref, x in zip(a_refs, around(place_ref, 1, X_CHIPS, X_RING)):
        for z in range(Z_CHIPS):
            for core in (0, 1):
                device = (z * X_CHIPS + x) * 2 + core
                to = pl.ds(pl.multiple_of(device * span, 16), span)
                piece = ref[2 * z + core]
                weight[to, pl.ds(0, split)] = piece[:span]
                query_out[device] = piece[span:].astype(jnp.float32)
    for ref, z in zip(b_refs, around(place_ref, 0, Z_CHIPS, Z_RING)):
        to = pl.ds(pl.multiple_of(z * features, 16), features)
        weight[to, pl.ds(split, width - split)] = ref[...]

    chunk = 1024 if depth % 1024 == 0 else depth
    for part, (rows_ref, out) in enumerate(((own_ref, own_out), (other_ref, other_out))):
        span = pl.ds(part * rows, rows)
        total = jnp.zeros((rows, width), jnp.float32)
        for k in range(depth // chunk):
            lanes = pl.ds(k * chunk, chunk)
            total += jnp.dot(
                rows_ref[:, lanes], weight[lanes, :], preferred_element_type=jnp.float32
            )
        cosine, sine = cos_ref[span, :], sin_ref[span, :]
        for head in range(width // HEAD_DIM):
            value = total[:, head * HEAD_DIM : (head + 1) * HEAD_DIM]
            turned = value * cosine + pltpu.roll(value, HEAD_DIM // 2, 1) * sine
            out[:, pl.ds(head * HEAD_DIM, HEAD_DIM)] = turned.astype(out.dtype)


def project(place, own, other, cosine, sine, a_blocks, b_blocks):
    rows, depth = own.shape
    split = a_blocks[0].shape[2]
    width = split + b_blocks[0].shape[1]
    lines = a_blocks[0].shape[1] - depth // (2 * Z_CHIPS * X_CHIPS)
    out = jax.ShapeDtypeStruct((rows, width), jnp.bfloat16)
    notes = jax.ShapeDtypeStruct((2 * Z_CHIPS * X_CHIPS, lines, split), jnp.float32)
    vmem = pl.BlockSpec(memory_space=pltpu.VMEM)
    operands = (own, other, cosine, sine, *a_blocks, *b_blocks)
    return pl.pallas_call(
        project_kernel,
        in_specs=[pl.BlockSpec(memory_space=pltpu.SMEM)] + [vmem] * len(operands),
        out_specs=[vmem] * 3,
        out_shape=[out, out, notes],
        scratch_shapes=[pltpu.VMEM((depth, width), jnp.bfloat16)],
        compiler_params=pltpu.CompilerParams(vmem_limit_bytes=40 * MIB),
        cost_estimate=pl.CostEstimate(
            flops=4 * rows * depth * width,
            bytes_accessed=4 * rows * depth + 2 * depth * width,
            transcendentals=0,
        ),
    )(place, *operands)


def attend_kernel(place_ref, mine_ref, theirs_ref, query_ref, keys_ref, out_ref, tiles):
    has_keys = place_ref[2] == 0
    count = query_ref.shape[0]
    heads = mine_ref.shape[1] // HEAD_DIM
    key_conv = keys_ref[0:1, :]

    def rows_of(part):
        return query_ref[:, part // 2, pl.ds(part % 2 * HEAD_DIM, HEAD_DIM)]

    allowed = rows_of(heads)[:, 0:1] == key_conv
    lane = lax.broadcasted_iota(jnp.int32, (count, HEAD_DIM), 1)
    stats = jnp.zeros(lane.shape, jnp.float32)
    for head in range(heads):
        lanes = pl.ds(head * HEAD_DIM, HEAD_DIM)
        mine, theirs = mine_ref[:, lanes], theirs_ref[:, lanes]
        keys = jnp.where(has_keys, mine, theirs)
        values = jnp.where(has_keys, theirs, mine)
        scores = lax.dot_general(
            rows_of(head).astype(jnp.bfloat16),
            keys,
            (((1,), (1,)), ((), ())),
            preferred_element_type=jnp.float32,
        )
        scores = jnp.where(allowed, scores * (1.0 / math.sqrt(HEAD_DIM)), NEG_FILL)
        top = jnp.max(scores, axis=-1, keepdims=True)
        weight = jnp.where(allowed, jnp.exp(scores - top), 0.0).astype(jnp.bfloat16)
        total = jnp.sum(weight.astype(jnp.float32), axis=-1, keepdims=True)
        tiles[:, head, :] = jnp.dot(weight, values, preferred_element_type=jnp.float32)
        at = head
        for value, parts in ((top, TOP_PARTS), (total, SUM_PARTS)):
            for _ in range(parts):
                rounded = value.astype(jnp.bfloat16).astype(jnp.float32)
                stats = jnp.where(lane == at, rounded, stats)
                value = value - rounded
                at += 8
    tiles[:, heads, :] = stats
    for row in range(heads + 1, 8):
        tiles[:, row, :] = jnp.zeros_like(stats)
    out_ref[...] = tiles[...].astype(jnp.bfloat16)


def attend(place, mine, theirs, queries, key_conv):
    shape = (queries.shape[0], 8, HEAD_DIM)
    vmem = pl.BlockSpec(memory_space=pltpu.VMEM)
    return pl.pallas_call(
        attend_kernel,
        in_specs=[pl.BlockSpec(memory_space=pltpu.SMEM)] + [vmem] * 4,
        out_specs=vmem,
        out_shape=jax.ShapeDtypeStruct(shape, jnp.bfloat16),
        scratch_shapes=[pltpu.VMEM(shape, jnp.float32)],
        compiler_params=pltpu.CompilerParams(vmem_limit_bytes=16 * MIB),
    )(place, mine, theirs, queries, key_conv)


def merge_kernel(heads, parts_ref, query_ref, new_ref, out_ref, parts, tile):
    parts[...] = parts_ref[...].astype(jnp.float32)
    stats = parts[:, heads, :]
    tile[...] = jnp.zeros_like(tile)
    for head in range(heads):
        lanes = pl.ds(head * HEAD_DIM, HEAD_DIM)
        query = query_ref[:, lanes].astype(jnp.float32)
        own_key = new_ref[0:1, lanes].astype(jnp.float32)
        own_value = new_ref[1:2, lanes].astype(jnp.float32)
        own = jnp.sum(query * own_key, axis=-1, keepdims=True) * (1.0 / math.sqrt(HEAD_DIM))
        stat = [stats[:, head + 8 * k : head + 8 * k + 1] for k in range(TOP_PARTS + SUM_PARTS)]
        top, total = sum(stat[1:TOP_PARTS], stat[0]), sum(stat[TOP_PARTS + 1 :], stat[TOP_PARTS])
        best = jnp.maximum(jnp.max(top, axis=0, keepdims=True), own)
        factor = jnp.exp(top - best)
        own_weight = jnp.exp(own - best).astype(jnp.bfloat16).astype(jnp.float32)
        total = jnp.sum(total * factor, axis=0, keepdims=True) + own_weight
        mixed = jnp.sum(parts[:, head, :] * factor, axis=0, keepdims=True)
        tile[head : head + 1, :] = (mixed + own_weight * own_value) / total
    out_ref[...] = jnp.broadcast_to(tile[...].astype(jnp.bfloat16), out_ref.shape)


def merge(parts, query, new_pair):
    vmem = pl.BlockSpec(memory_space=pltpu.VMEM)
    return pl.pallas_call(
        functools.partial(merge_kernel, query.shape[1] // HEAD_DIM),
        in_specs=[vmem] * 3,
        out_specs=vmem,
        out_shape=jax.ShapeDtypeStruct(parts.shape, jnp.bfloat16),
        scratch_shapes=[
            pltpu.VMEM(parts.shape, jnp.float32),
            pltpu.VMEM(parts.shape[1:], jnp.float32),
        ],
        compiler_params=pltpu.CompilerParams(vmem_limit_bytes=16 * MIB),
    )(parts, query, new_pair)


def send(value, dz, dx):
    pairs = []
    for z in range(Z_CHIPS):
        for x in range(X_CHIPS):
            for core, sign in ((0, 1), (1, -1)):
                to = ((z + sign * dz) % Z_CHIPS * X_CHIPS + (x + sign * dx) % X_CHIPS) * 2 + core
                pairs.append(((z * X_CHIPS + x) * 2 + core, to))
    return lax.ppermute(value, GROUP, pairs)


def exchange(value, axis):
    return lax.all_to_all(value, axis, 0, 0, tiled=True)


def per_device(
    saved, block_per_slot, lengths, norm_gain, kv_weight, out_weight, queries, new_kv, row_conv
):
    slot_dev, block_rows, model_width = saved.shape
    groups = lax.axis_size(GROUP)
    blocks_conv = slot_dev * groups // lengths.shape[0]
    local_width = kv_weight.shape[2]
    heads = local_width // HEAD_DIM
    core = lax.axis_index("core")
    first_core = core == 0

    split = 2 * HEAD_DIM
    def copies(pieces, chips):
        pieces = jnp.broadcast_to(jnp.stack(pieces), (chips, 2) + pieces[0].shape)
        return pieces.reshape(-1, *pieces.shape[2:])

    part_rows = kv_weight.shape[0]
    block_b = exchange(copies([kv_weight[:, k, split:] for k in (0, 1)], X_CHIPS), ("x", "core"))
    block_b = block_b.reshape(-1, local_width - split)
    numbers = jnp.concatenate([row_conv, block_per_slot]).astype(jnp.bfloat16)
    numbers = jnp.broadcast_to(numbers[:, None], (1 + slot_dev, split))
    wide = jnp.concatenate([queries, numbers[:1, :HEAD_DIM]], axis=1)
    lines = [wide[:, at : at + split] for at in range(0, wide.shape[1], split)]
    notes = jnp.concatenate([*lines, numbers[1:]])
    notes = jnp.pad(notes, ((0, 8 - notes.shape[0]), (0, 0)))
    pieces_a = [jnp.concatenate([kv_weight[:, k, :split], notes]) for k in (0, 1)]
    copies_a = copies(pieces_a, Z_CHIPS)
    pieces_a = exchange(copies_a, ("z", "core"))
    saved, block_b, _ = lax.optimization_barrier((saved, block_b, copies_a))
    a_behind, a_ahead = send(pieces_a, 0, 1), send(pieces_a, 0, -1)
    behind1, ahead1 = send(block_b, 1, 0), send(block_b, -1, 0)
    behind1, ahead1 = lax.optimization_barrier((behind1, ahead1))
    ahead1, a_behind = lax.optimization_barrier((ahead1, a_behind))
    behind2, ahead2 = send(behind1, 1, 0), send(ahead1, -1, 0)
    ahead2, a_ahead = lax.optimization_barrier((ahead2, a_ahead))
    behind3, ahead3 = send(behind2, 1, 0), send(ahead2, -1, 0)
    a_blocks = (pieces_a, a_behind, a_ahead, send(a_behind, 0, 1))
    b_blocks = (block_b, behind1, ahead1, behind2, ahead2, behind3, ahead3, send(behind3, 1, 0))

    normed = normalize(saved, norm_gain).reshape(slot_dev * block_rows, model_width)
    other_normed = swap_cores(normed)
    beside = 2 * lax.axis_index("z") + 1 - core
    other_blocks = lax.dynamic_index_in_dim(pieces_a, beside, keepdims=False)
    first_line = part_rows + len(lines)
    other_blocks = other_blocks[first_line : first_line + slot_dev, 0]
    blocks = jnp.concatenate([block_per_slot, other_blocks.astype(jnp.int32)])
    conv = blocks // blocks_conv
    positions = (blocks % blocks_conv * block_rows)[:, None] + jnp.arange(
        block_rows, dtype=jnp.int32
    )
    live = (positions < lookup(lengths, conv)[:, None]).reshape(-1, 1)
    half_dim = HEAD_DIM // 2
    freq_index = jnp.arange(half_dim, dtype=jnp.float32)
    inverse = jnp.exp(freq_index * (-2.0 * math.log(10000.0) / HEAD_DIM))
    angles = positions.reshape(-1, 1).astype(jnp.float32) * inverse
    cosine, sine = jnp.cos(angles), jnp.sin(angles)
    cosine = jnp.where(first_core, jnp.concatenate([cosine, cosine], axis=-1), 1.0)
    sine = jnp.where(first_core, jnp.concatenate([-sine, sine], axis=-1), 0.0)
    cosine, sine = jnp.where(live, cosine, 0.0), jnp.where(live, sine, 0.0)
    own_rows = slot_dev * block_rows
    key_conv = jnp.where(live[:own_rows, 0], jnp.repeat(conv[:slot_dev], block_rows), -1)
    key_conv = jnp.broadcast_to(key_conv.astype(jnp.float32), (8, own_rows))
    place = jnp.stack([lax.axis_index("z"), lax.axis_index("x"), core]).astype(jnp.int32)

    mine, give, tiles = project(
        place, normed, other_normed, cosine, sine, a_blocks, b_blocks
    )
    theirs = swap_cores(give)
    parts = attend(place, mine, theirs, tiles, key_conv)
    merged = merge(exchange(parts, GROUP), queries, new_kv[0])
    attended = exchange(merged, GROUP)[:, :heads].reshape(groups, local_width)
    decoded = jnp.dot(attended, out_weight, preferred_element_type=jnp.float32)
    tp = lax.axis_size("tp")
    decoded = exchange(decoded.reshape(tp, groups // tp, -1), "tp")
    decoded = jnp.sum(decoded, axis=0).astype(jnp.bfloat16)

    keys = jnp.where(first_core, mine, theirs)
    values = jnp.where(first_core, theirs, mine)
    kv_cache = jnp.stack([keys, values], axis=1).reshape(slot_dev, block_rows, 2, local_width)
    return (kv_cache, decoded)


def solution(mesh):
    groups, tp = mesh.devices.shape
    fine = Mesh(
        mesh.devices.reshape(Z_CHIPS, X_CHIPS, groups // (Z_CHIPS * X_CHIPS), tp), GROUP + ("tp",)
    )
    placed = (
        P(GROUP, None, None),
        P(GROUP),
        P(),
        P(),
        P(GROUP, None, "tp"),
        P("tp", GROUP),
        P(GROUP, "tp"),
        P(GROUP, None, "tp"),
        P(GROUP),
    )
    return jax.shard_map(
        per_device,
        mesh=fine,
        in_specs=placed,
        out_specs=(P(GROUP, None, None, "tp"), P("tp", GROUP)),
        check_vma=False,
    )
```

```python
import functools
import math

import jax
import jax.numpy as jnp
from jax import lax
from jax.experimental import pallas as pl
from jax.experimental.pallas import tpu as pltpu
from jax.sharding import Mesh
from jax.sharding import PartitionSpec as P

HEAD_DIM = 128
EPSILON = 1e-05
NEG_FILL = -1e30
GROUP = ("z", "x", "core")
MIB = 1 << 20
Z_CHIPS, X_CHIPS = 8, 4
Z_RING, X_RING = (0, -1, 1, -2, 2, -3, 3, 4), (0, -1, 1, 2)
TOP_PARTS, SUM_PARTS = 3, 2


def normalize(saved_rows, norm_gain):
    as_float = saved_rows.astype(jnp.float32)
    inv_rms = lax.rsqrt(jnp.mean(as_float * as_float, axis=-1, keepdims=True) + EPSILON)
    return (as_float * inv_rms * norm_gain.astype(jnp.float32)).astype(jnp.bfloat16)


def lookup(lookup_table, indices):
    matches = indices[..., None] == jnp.arange(lookup_table.shape[0], dtype=jnp.int32)
    return jnp.sum(jnp.where(matches, lookup_table, 0), axis=-1)


def swap_cores(value):
    return lax.ppermute(value, "core", [(0, 1), (1, 0)])


def around(place_ref, axis, chips, ring):
    sign = 1 - 2 * place_ref[2]
    return [lax.rem(place_ref[axis] + sign * step + chips, chips) for step in ring]


def project_kernel(place_ref, own_ref, other_ref, cos_ref, sin_ref, *refs):
    a_refs, b_refs = refs[: len(X_RING)], refs[len(X_RING) : len(X_RING) + len(Z_RING)]
    own_out, other_out, query_out, weight = refs[len(X_RING) + len(Z_RING) :]
    rows, depth = own_ref.shape
    width = weight.shape[1]
    devices, split = query_out.shape[0], query_out.shape[2]
    span, features = depth // devices, b_refs[0].shape[0]

    for ref, x in zip(a_refs, around(place_ref, 1, X_CHIPS, X_RING)):
        for z in range(Z_CHIPS):
            for core in (0, 1):
                device = (z * X_CHIPS + x) * 2 + core
                to = pl.ds(pl.multiple_of(device * span, 16), span)
                piece = ref[2 * z + core]
                weight[to, pl.ds(0, split)] = piece[:span]
                query_out[device] = piece[span:].astype(jnp.float32)
    for ref, z in zip(b_refs, around(place_ref, 0, Z_CHIPS, Z_RING)):
        to = pl.ds(pl.multiple_of(z * features, 16), features)
        weight[to, pl.ds(split, width - split)] = ref[...]

    chunk = 1024 if depth % 1024 == 0 else depth
    for part, (rows_ref, out) in enumerate(((own_ref, own_out), (other_ref, other_out))):
        span = pl.ds(part * rows, rows)
        total = jnp.zeros((rows, width), jnp.float32)
        for k in range(depth // chunk):
            lanes = pl.ds(k * chunk, chunk)
            total += jnp.dot(
                rows_ref[:, lanes], weight[lanes, :], preferred_element_type=jnp.float32
            )
        cosine, sine = cos_ref[span, :], sin_ref[span, :]
        for head in range(width // HEAD_DIM):
            value = total[:, head * HEAD_DIM : (head + 1) * HEAD_DIM]
            turned = value * cosine + pltpu.roll(value, HEAD_DIM // 2, 1) * sine
            out[:, pl.ds(head * HEAD_DIM, HEAD_DIM)] = turned.astype(out.dtype)


def project(place, own, other, cosine, sine, a_blocks, b_blocks):
    rows, depth = own.shape
    split = a_blocks[0].shape[2]
    width = split + b_blocks[0].shape[1]
    lines = a_blocks[0].shape[1] - depth // (2 * Z_CHIPS * X_CHIPS)
    out = jax.ShapeDtypeStruct((rows, width), jnp.bfloat16)
    notes = jax.ShapeDtypeStruct((2 * Z_CHIPS * X_CHIPS, lines, split), jnp.float32)
    vmem = pl.BlockSpec(memory_space=pltpu.VMEM)
    operands = (own, other, cosine, sine, *a_blocks, *b_blocks)
    return pl.pallas_call(
        project_kernel,
        in_specs=[pl.BlockSpec(memory_space=pltpu.SMEM)] + [vmem] * len(operands),
        out_specs=[vmem] * 3,
        out_shape=[out, out, notes],
        scratch_shapes=[pltpu.VMEM((depth, width), jnp.bfloat16)],
        compiler_params=pltpu.CompilerParams(vmem_limit_bytes=40 * MIB),
        cost_estimate=pl.CostEstimate(
            flops=4 * rows * depth * width,
            bytes_accessed=4 * rows * depth + 2 * depth * width,
            transcendentals=0,
        ),
    )(place, *operands)


def attend_kernel(place_ref, mine_ref, theirs_ref, query_ref, keys_ref, out_ref, tiles):
    has_keys = place_ref[2] == 0
    count = query_ref.shape[0]
    heads = mine_ref.shape[1] // HEAD_DIM
    key_conv = keys_ref[0:1, :]

    def rows_of(part):
        return query_ref[:, part // 2, pl.ds(part % 2 * HEAD_DIM, HEAD_DIM)]

    allowed = rows_of(heads)[:, 0:1] == key_conv
    lane = lax.broadcasted_iota(jnp.int32, (count, HEAD_DIM), 1)
    stats = jnp.zeros(lane.shape, jnp.float32)
    for head in range(heads):
        lanes = pl.ds(head * HEAD_DIM, HEAD_DIM)
        mine, theirs = mine_ref[:, lanes], theirs_ref[:, lanes]
        keys = jnp.where(has_keys, mine, theirs)
        values = jnp.where(has_keys, theirs, mine)
        scores = lax.dot_general(
            rows_of(head).astype(jnp.bfloat16),
            keys,
            (((1,), (1,)), ((), ())),
            preferred_element_type=jnp.float32,
        )
        scores = jnp.where(allowed, scores * (1.0 / math.sqrt(HEAD_DIM)), NEG_FILL)
        top = jnp.max(scores, axis=-1, keepdims=True)
        weight = jnp.where(allowed, jnp.exp(scores - top), 0.0).astype(jnp.bfloat16)
        total = jnp.sum(weight.astype(jnp.float32), axis=-1, keepdims=True)
        tiles[:, head, :] = jnp.dot(weight, values, preferred_element_type=jnp.float32)
        at = head
        for value, parts in ((top, TOP_PARTS), (total, SUM_PARTS)):
            for _ in range(parts):
                rounded = value.astype(jnp.bfloat16).astype(jnp.float32)
                stats = jnp.where(lane == at, rounded, stats)
                value = value - rounded
                at += 8
    tiles[:, heads, :] = stats
    for row in range(heads + 1, 8):
        tiles[:, row, :] = jnp.zeros_like(stats)
    out_ref[...] = tiles[...].astype(jnp.bfloat16)


def attend(place, mine, theirs, queries, key_conv):
    shape = (queries.shape[0], 8, HEAD_DIM)
    vmem = pl.BlockSpec(memory_space=pltpu.VMEM)
    return pl.pallas_call(
        attend_kernel,
        in_specs=[pl.BlockSpec(memory_space=pltpu.SMEM)] + [vmem] * 4,
        out_specs=vmem,
        out_shape=jax.ShapeDtypeStruct(shape, jnp.bfloat16),
        scratch_shapes=[pltpu.VMEM(shape, jnp.float32)],
        compiler_params=pltpu.CompilerParams(vmem_limit_bytes=16 * MIB),
    )(place, mine, theirs, queries, key_conv)


def merge_kernel(heads, parts_ref, query_ref, new_ref, out_ref, parts, tile):
    parts[...] = parts_ref[...].astype(jnp.float32)
    stats = parts[:, heads, :]
    tile[...] = jnp.zeros_like(tile)
    for head in range(heads):
        lanes = pl.ds(head * HEAD_DIM, HEAD_DIM)
        query = query_ref[:, lanes].astype(jnp.float32)
        own_key = new_ref[0:1, lanes].astype(jnp.float32)
        own_value = new_ref[1:2, lanes].astype(jnp.float32)
        own = jnp.sum(query * own_key, axis=-1, keepdims=True) * (1.0 / math.sqrt(HEAD_DIM))
        stat = [stats[:, head + 8 * k : head + 8 * k + 1] for k in range(TOP_PARTS + SUM_PARTS)]
        top, total = sum(stat[1:TOP_PARTS], stat[0]), sum(stat[TOP_PARTS + 1 :], stat[TOP_PARTS])
        best = jnp.maximum(jnp.max(top, axis=0, keepdims=True), own)
        factor = jnp.exp(top - best)
        own_weight = jnp.exp(own - best).astype(jnp.bfloat16).astype(jnp.float32)
        total = jnp.sum(total * factor, axis=0, keepdims=True) + own_weight
        mixed = jnp.sum(parts[:, head, :] * factor, axis=0, keepdims=True)
        tile[head : head + 1, :] = (mixed + own_weight * own_value) / total
    out_ref[...] = jnp.broadcast_to(tile[...].astype(jnp.bfloat16), out_ref.shape)


def merge(parts, query, new_pair):
    vmem = pl.BlockSpec(memory_space=pltpu.VMEM)
    return pl.pallas_call(
        functools.partial(merge_kernel, query.shape[1] // HEAD_DIM),
        in_specs=[vmem] * 3,
        out_specs=vmem,
        out_shape=jax.ShapeDtypeStruct(parts.shape, jnp.bfloat16),
        scratch_shapes=[
            pltpu.VMEM(parts.shape, jnp.float32),
            pltpu.VMEM(parts.shape[1:], jnp.float32),
        ],
        compiler_params=pltpu.CompilerParams(vmem_limit_bytes=16 * MIB),
    )(parts, query, new_pair)


def send(value, dz, dx):
    pairs = []
    for z in range(Z_CHIPS):
        for x in range(X_CHIPS):
            for core, sign in ((0, 1), (1, -1)):
                to = ((z + sign * dz) % Z_CHIPS * X_CHIPS + (x + sign * dx) % X_CHIPS) * 2 + core
                pairs.append(((z * X_CHIPS + x) * 2 + core, to))
    return lax.ppermute(value, GROUP, pairs)


def exchange(value, axis):
    return lax.all_to_all(value, axis, 0, 0, tiled=True)


def per_device(
    saved, block_per_slot, lengths, norm_gain, kv_weight, out_weight, queries, new_kv, row_conv
):
    slot_dev, block_rows, model_width = saved.shape
    groups = lax.axis_size(GROUP)
    blocks_conv = slot_dev * groups // lengths.shape[0]
    local_width = kv_weight.shape[2]
    heads = local_width // HEAD_DIM
    core = lax.axis_index("core")
    first_core = core == 0

    split = 2 * HEAD_DIM
    def copies(pieces, chips):
        pieces = jnp.broadcast_to(jnp.stack(pieces), (chips, 2) + pieces[0].shape)
        return pieces.reshape(-1, *pieces.shape[2:])

    part_rows = kv_weight.shape[0]
    block_b = exchange(copies([kv_weight[:, k, split:] for k in (0, 1)], X_CHIPS), ("x", "core"))
    block_b = block_b.reshape(-1, local_width - split)
    numbers = jnp.concatenate([row_conv, block_per_slot]).astype(jnp.bfloat16)
    numbers = jnp.broadcast_to(numbers[:, None], (1 + slot_dev, split))
    wide = jnp.concatenate([queries, numbers[:1, :HEAD_DIM]], axis=1)
    lines = [wide[:, at : at + split] for at in range(0, wide.shape[1], split)]
    notes = jnp.concatenate([*lines, numbers[1:]])
    notes = jnp.pad(notes, ((0, 8 - notes.shape[0]), (0, 0)))
    pieces_a = [jnp.concatenate([kv_weight[:, k, :split], notes]) for k in (0, 1)]
    copies_a = copies(pieces_a, Z_CHIPS)
    pieces_a = exchange(copies_a, ("z", "core"))
    saved, block_b, _ = lax.optimization_barrier((saved, block_b, copies_a))
    a_behind, a_ahead = send(pieces_a, 0, 1), send(pieces_a, 0, -1)
    behind1, ahead1 = send(block_b, 1, 0), send(block_b, -1, 0)
    behind2, ahead2 = send(behind1, 1, 0), send(ahead1, -1, 0)
    behind3, ahead3 = send(behind2, 1, 0), send(ahead2, -1, 0)
    behind3, a_last = lax.optimization_barrier((behind3, send(a_behind, 0, 1)))
    a_blocks = (pieces_a, a_behind, a_ahead, a_last)
    b_blocks = (block_b, behind1, ahead1, behind2, ahead2, behind3, ahead3, send(behind3, 1, 0))

    normed = normalize(saved, norm_gain).reshape(slot_dev * block_rows, model_width)
    other_normed = swap_cores(normed)
    beside = 2 * lax.axis_index("z") + 1 - core
    other_blocks = lax.dynamic_index_in_dim(pieces_a, beside, keepdims=False)
    first_line = part_rows + len(lines)
    other_blocks = other_blocks[first_line : first_line + slot_dev, 0]
    blocks = jnp.concatenate([block_per_slot, other_blocks.astype(jnp.int32)])
    conv = blocks // blocks_conv
    positions = (blocks % blocks_conv * block_rows)[:, None] + jnp.arange(
        block_rows, dtype=jnp.int32
    )
    live = (positions < lookup(lengths, conv)[:, None]).reshape(-1, 1)
    half_dim = HEAD_DIM // 2
    freq_index = jnp.arange(half_dim, dtype=jnp.float32)
    inverse = jnp.exp(freq_index * (-2.0 * math.log(10000.0) / HEAD_DIM))
    angles = positions.reshape(-1, 1).astype(jnp.float32) * inverse
    cosine, sine = jnp.cos(angles), jnp.sin(angles)
    cosine = jnp.where(first_core, jnp.concatenate([cosine, cosine], axis=-1), 1.0)
    sine = jnp.where(first_core, jnp.concatenate([-sine, sine], axis=-1), 0.0)
    cosine, sine = jnp.where(live, cosine, 0.0), jnp.where(live, sine, 0.0)
    own_rows = slot_dev * block_rows
    key_conv = jnp.where(live[:own_rows, 0], jnp.repeat(conv[:slot_dev], block_rows), -1)
    key_conv = jnp.broadcast_to(key_conv.astype(jnp.float32), (8, own_rows))
    place = jnp.stack([lax.axis_index("z"), lax.axis_index("x"), core]).astype(jnp.int32)

    mine, give, tiles = project(
        place, normed, other_normed, cosine, sine, a_blocks, b_blocks
    )
    theirs = swap_cores(give)
    parts = attend(place, mine, theirs, tiles, key_conv)
    merged = merge(exchange(parts, GROUP), queries, new_kv[0])
    attended = exchange(merged, GROUP)[:, :heads].reshape(groups, local_width)
    decoded = jnp.dot(attended, out_weight, preferred_element_type=jnp.float32)
    tp = lax.axis_size("tp")
    decoded = exchange(decoded.reshape(tp, groups // tp, -1), "tp")
    decoded = jnp.sum(decoded, axis=0).astype(jnp.bfloat16)

    keys = jnp.where(first_core, mine, theirs)
    values = jnp.where(first_core, theirs, mine)
    kv_cache = jnp.stack([keys, values], axis=1).reshape(slot_dev, block_rows, 2, local_width)
    return (kv_cache, decoded)


def solution(mesh):
    groups, tp = mesh.devices.shape
    fine = Mesh(
        mesh.devices.reshape(Z_CHIPS, X_CHIPS, groups // (Z_CHIPS * X_CHIPS), tp), GROUP + ("tp",)
    )
    placed = (
        P(GROUP, None, None),
        P(GROUP),
        P(),
        P(),
        P(GROUP, None, "tp"),
        P("tp", GROUP),
        P(GROUP, "tp"),
        P(GROUP, None, "tp"),
        P(GROUP),
    )
    return jax.shard_map(
        per_device,
        mesh=fine,
        in_specs=placed,
        out_specs=(P(GROUP, None, None, "tp"), P("tp", GROUP)),
        check_vma=False,
    )
```

```python
import functools
import math

import jax
import jax.numpy as jnp
from jax import lax
from jax.experimental import pallas as pl
from jax.experimental.pallas import tpu as pltpu
from jax.sharding import Mesh
from jax.sharding import PartitionSpec as P

HEAD_DIM = 128
EPSILON = 1e-05
NEG_FILL = -1e30
GROUP = ("z", "x", "core")
MIB = 1 << 20
Z_CHIPS, X_CHIPS = 8, 4
Z_RING, X_RING = (0, -1, 1, -2, 2, -3, 3, 4), (0, -1, 1, 2)
TOP_PARTS, SUM_PARTS = 3, 2


def normalize(saved_rows, norm_gain):
    as_float = saved_rows.astype(jnp.float32)
    inv_rms = lax.rsqrt(jnp.mean(as_float * as_float, axis=-1, keepdims=True) + EPSILON)
    return (as_float * inv_rms * norm_gain.astype(jnp.float32)).astype(jnp.bfloat16)


def lookup(lookup_table, indices):
    matches = indices[..., None] == jnp.arange(lookup_table.shape[0], dtype=jnp.int32)
    return jnp.sum(jnp.where(matches, lookup_table, 0), axis=-1)


def swap_cores(value):
    return lax.ppermute(value, "core", [(0, 1), (1, 0)])


def around(place_ref, axis, chips, ring):
    sign = 1 - 2 * place_ref[2]
    return [lax.rem(place_ref[axis] + sign * step + chips, chips) for step in ring]


def project_kernel(place_ref, own_ref, other_ref, cos_ref, sin_ref, *refs):
    a_refs, b_refs = refs[: len(X_RING)], refs[len(X_RING) : len(X_RING) + len(Z_RING)]
    own_out, other_out, query_out, weight = refs[len(X_RING) + len(Z_RING) :]
    rows, depth = own_ref.shape
    width = weight.shape[1]
    devices, split = query_out.shape[0], query_out.shape[2]
    span, features = depth // devices, b_refs[0].shape[0]

    for ref, x in zip(a_refs, around(place_ref, 1, X_CHIPS, X_RING)):
        for z in range(Z_CHIPS):
            for core in (0, 1):
                device = (z * X_CHIPS + x) * 2 + core
                to = pl.ds(pl.multiple_of(device * span, 16), span)
                piece = ref[2 * z + core]
                weight[to, pl.ds(0, split)] = piece[:span]
                query_out[device] = piece[span:].astype(jnp.float32)
    for ref, z in zip(b_refs, around(place_ref, 0, Z_CHIPS, Z_RING)):
        to = pl.ds(pl.multiple_of(z * features, 16), features)
        weight[to, pl.ds(split, width - split)] = ref[...]

    chunk = 1024 if depth % 1024 == 0 else depth
    both = jnp.zeros((2 * rows, width), jnp.float32)
    for k in range(depth // chunk):
        lanes = pl.ds(k * chunk, chunk)
        stacked = jnp.concatenate([own_ref[:, lanes], other_ref[:, lanes]])
        both += jnp.dot(stacked, weight[lanes, :], preferred_element_type=jnp.float32)
    for part, out in enumerate((own_out, other_out)):
        span = pl.ds(part * rows, rows)
        total = both[part * rows : (part + 1) * rows]
        cosine, sine = cos_ref[span, :], sin_ref[span, :]
        for head in range(width // HEAD_DIM):
            value = total[:, head * HEAD_DIM : (head + 1) * HEAD_DIM]
            turned = value * cosine + pltpu.roll(value, HEAD_DIM // 2, 1) * sine
            out[:, pl.ds(head * HEAD_DIM, HEAD_DIM)] = turned.astype(out.dtype)


def project(place, own, other, cosine, sine, a_blocks, b_blocks):
    rows, depth = own.shape
    split = a_blocks[0].shape[2]
    width = split + b_blocks[0].shape[1]
    lines = a_blocks[0].shape[1] - depth // (2 * Z_CHIPS * X_CHIPS)
    out = jax.ShapeDtypeStruct((rows, width), jnp.bfloat16)
    notes = jax.ShapeDtypeStruct((2 * Z_CHIPS * X_CHIPS, lines, split), jnp.float32)
    vmem = pl.BlockSpec(memory_space=pltpu.VMEM)
    operands = (own, other, cosine, sine, *a_blocks, *b_blocks)
    return pl.pallas_call(
        project_kernel,
        in_specs=[pl.BlockSpec(memory_space=pltpu.SMEM)] + [vmem] * len(operands),
        out_specs=[vmem] * 3,
        out_shape=[out, out, notes],
        scratch_shapes=[pltpu.VMEM((depth, width), jnp.bfloat16)],
        compiler_params=pltpu.CompilerParams(vmem_limit_bytes=40 * MIB),
        cost_estimate=pl.CostEstimate(
            flops=4 * rows * depth * width,
            bytes_accessed=4 * rows * depth + 2 * depth * width,
            transcendentals=0,
        ),
    )(place, *operands)


def attend_kernel(place_ref, mine_ref, theirs_ref, query_ref, keys_ref, out_ref, tiles):
    has_keys = place_ref[2] == 0
    count = query_ref.shape[0]
    heads = mine_ref.shape[1] // HEAD_DIM
    key_conv = keys_ref[0:1, :]

    def rows_of(part):
        return query_ref[:, part // 2, pl.ds(part % 2 * HEAD_DIM, HEAD_DIM)]

    allowed = rows_of(heads)[:, 0:1] == key_conv
    lane = lax.broadcasted_iota(jnp.int32, (count, HEAD_DIM), 1)
    stats = jnp.zeros(lane.shape, jnp.float32)
    for head in range(heads):
        lanes = pl.ds(head * HEAD_DIM, HEAD_DIM)
        mine, theirs = mine_ref[:, lanes], theirs_ref[:, lanes]
        keys = jnp.where(has_keys, mine, theirs)
        values = jnp.where(has_keys, theirs, mine)
        scores = lax.dot_general(
            rows_of(head).astype(jnp.bfloat16),
            keys,
            (((1,), (1,)), ((), ())),
            preferred_element_type=jnp.float32,
        )
        scores = jnp.where(allowed, scores * (1.0 / math.sqrt(HEAD_DIM)), NEG_FILL)
        top = jnp.max(scores, axis=-1, keepdims=True)
        weight = jnp.where(allowed, jnp.exp(scores - top), 0.0).astype(jnp.bfloat16)
        total = jnp.sum(weight.astype(jnp.float32), axis=-1, keepdims=True)
        tiles[:, head, :] = jnp.dot(weight, values, preferred_element_type=jnp.float32)
        at = head
        for value, parts in ((top, TOP_PARTS), (total, SUM_PARTS)):
            for _ in range(parts):
                rounded = value.astype(jnp.bfloat16).astype(jnp.float32)
                stats = jnp.where(lane == at, rounded, stats)
                value = value - rounded
                at += 8
    tiles[:, heads, :] = stats
    for row in range(heads + 1, 8):
        tiles[:, row, :] = jnp.zeros_like(stats)
    out_ref[...] = tiles[...].astype(jnp.bfloat16)


def attend(place, mine, theirs, queries, key_conv):
    shape = (queries.shape[0], 8, HEAD_DIM)
    vmem = pl.BlockSpec(memory_space=pltpu.VMEM)
    return pl.pallas_call(
        attend_kernel,
        in_specs=[pl.BlockSpec(memory_space=pltpu.SMEM)] + [vmem] * 4,
        out_specs=vmem,
        out_shape=jax.ShapeDtypeStruct(shape, jnp.bfloat16),
        scratch_shapes=[pltpu.VMEM(shape, jnp.float32)],
        compiler_params=pltpu.CompilerParams(vmem_limit_bytes=16 * MIB),
    )(place, mine, theirs, queries, key_conv)


def merge_kernel(heads, parts_ref, query_ref, new_ref, out_ref, parts, tile):
    parts[...] = parts_ref[...].astype(jnp.float32)
    stats = parts[:, heads, :]
    tile[...] = jnp.zeros_like(tile)
    for head in range(heads):
        lanes = pl.ds(head * HEAD_DIM, HEAD_DIM)
        query = query_ref[:, lanes].astype(jnp.float32)
        own_key = new_ref[0:1, lanes].astype(jnp.float32)
        own_value = new_ref[1:2, lanes].astype(jnp.float32)
        own = jnp.sum(query * own_key, axis=-1, keepdims=True) * (1.0 / math.sqrt(HEAD_DIM))
        stat = [stats[:, head + 8 * k : head + 8 * k + 1] for k in range(TOP_PARTS + SUM_PARTS)]
        top, total = sum(stat[1:TOP_PARTS], stat[0]), sum(stat[TOP_PARTS + 1 :], stat[TOP_PARTS])
        best = jnp.maximum(jnp.max(top, axis=0, keepdims=True), own)
        factor = jnp.exp(top - best)
        own_weight = jnp.exp(own - best).astype(jnp.bfloat16).astype(jnp.float32)
        total = jnp.sum(total * factor, axis=0, keepdims=True) + own_weight
        mixed = jnp.sum(parts[:, head, :] * factor, axis=0, keepdims=True)
        tile[head : head + 1, :] = (mixed + own_weight * own_value) / total
    out_ref[...] = jnp.broadcast_to(tile[...].astype(jnp.bfloat16), out_ref.shape)


def merge(parts, query, new_pair):
    vmem = pl.BlockSpec(memory_space=pltpu.VMEM)
    return pl.pallas_call(
        functools.partial(merge_kernel, query.shape[1] // HEAD_DIM),
        in_specs=[vmem] * 3,
        out_specs=vmem,
        out_shape=jax.ShapeDtypeStruct(parts.shape, jnp.bfloat16),
        scratch_shapes=[
            pltpu.VMEM(parts.shape, jnp.float32),
            pltpu.VMEM(parts.shape[1:], jnp.float32),
        ],
        compiler_params=pltpu.CompilerParams(vmem_limit_bytes=16 * MIB),
    )(parts, query, new_pair)


def send(value, dz, dx):
    pairs = []
    for z in range(Z_CHIPS):
        for x in range(X_CHIPS):
            for core, sign in ((0, 1), (1, -1)):
                to = ((z + sign * dz) % Z_CHIPS * X_CHIPS + (x + sign * dx) % X_CHIPS) * 2 + core
                pairs.append(((z * X_CHIPS + x) * 2 + core, to))
    return lax.ppermute(value, GROUP, pairs)


def exchange(value, axis):
    return lax.all_to_all(value, axis, 0, 0, tiled=True)


def per_device(
    saved, block_per_slot, lengths, norm_gain, kv_weight, out_weight, queries, new_kv, row_conv
):
    slot_dev, block_rows, model_width = saved.shape
    groups = lax.axis_size(GROUP)
    blocks_conv = slot_dev * groups // lengths.shape[0]
    local_width = kv_weight.shape[2]
    heads = local_width // HEAD_DIM
    core = lax.axis_index("core")
    first_core = core == 0

    split = 2 * HEAD_DIM
    def copies(pieces, chips):
        pieces = jnp.broadcast_to(jnp.stack(pieces), (chips, 2) + pieces[0].shape)
        return pieces.reshape(-1, *pieces.shape[2:])

    part_rows = kv_weight.shape[0]
    block_b = exchange(copies([kv_weight[:, k, split:] for k in (0, 1)], X_CHIPS), ("x", "core"))
    block_b = block_b.reshape(-1, local_width - split)
    numbers = jnp.concatenate([row_conv, block_per_slot]).astype(jnp.bfloat16)
    numbers = jnp.broadcast_to(numbers[:, None], (1 + slot_dev, split))
    wide = jnp.concatenate([queries, numbers[:1, :HEAD_DIM]], axis=1)
    lines = [wide[:, at : at + split] for at in range(0, wide.shape[1], split)]
    notes = jnp.concatenate([*lines, numbers[1:]])
    notes = jnp.pad(notes, ((0, 8 - notes.shape[0]), (0, 0)))
    pieces_a = [jnp.concatenate([kv_weight[:, k, :split], notes]) for k in (0, 1)]
    copies_a = copies(pieces_a, Z_CHIPS)
    pieces_a = exchange(copies_a, ("z", "core"))
    saved, block_b, _ = lax.optimization_barrier((saved, block_b, copies_a))
    a_behind, a_ahead = send(pieces_a, 0, 1), send(pieces_a, 0, -1)
    behind1, ahead1 = send(block_b, 1, 0), send(block_b, -1, 0)
    ahead1, a_behind = lax.optimization_barrier((ahead1, a_behind))
    behind2, ahead2 = send(behind1, 1, 0), send(ahead1, -1, 0)
    ahead2, a_ahead = lax.optimization_barrier((ahead2, a_ahead))
    behind3, ahead3 = send(behind2, 1, 0), send(ahead2, -1, 0)
    a_blocks = (pieces_a, a_behind, a_ahead, send(a_behind, 0, 1))
    b_blocks = (block_b, behind1, ahead1, behind2, ahead2, behind3, ahead3, send(behind3, 1, 0))

    normed = normalize(saved, norm_gain).reshape(slot_dev * block_rows, model_width)
    other_normed = swap_cores(normed)
    beside = 2 * lax.axis_index("z") + 1 - core
    other_blocks = lax.dynamic_index_in_dim(pieces_a, beside, keepdims=False)
    first_line = part_rows + len(lines)
    other_blocks = other_blocks[first_line : first_line + slot_dev, 0]
    blocks = jnp.concatenate([block_per_slot, other_blocks.astype(jnp.int32)])
    conv = blocks // blocks_conv
    positions = (blocks % blocks_conv * block_rows)[:, None] + jnp.arange(
        block_rows, dtype=jnp.int32
    )
    live = (positions < lookup(lengths, conv)[:, None]).reshape(-1, 1)
    half_dim = HEAD_DIM // 2
    freq_index = jnp.arange(half_dim, dtype=jnp.float32)
    inverse = jnp.exp(freq_index * (-2.0 * math.log(10000.0) / HEAD_DIM))
    angles = positions.reshape(-1, 1).astype(jnp.float32) * inverse
    cosine, sine = jnp.cos(angles), jnp.sin(angles)
    cosine = jnp.where(first_core, jnp.concatenate([cosine, cosine], axis=-1), 1.0)
    sine = jnp.where(first_core, jnp.concatenate([-sine, sine], axis=-1), 0.0)
    cosine, sine = jnp.where(live, cosine, 0.0), jnp.where(live, sine, 0.0)
    own_rows = slot_dev * block_rows
    key_conv = jnp.where(live[:own_rows, 0], jnp.repeat(conv[:slot_dev], block_rows), -1)
    key_conv = jnp.broadcast_to(key_conv.astype(jnp.float32), (8, own_rows))
    place = jnp.stack([lax.axis_index("z"), lax.axis_index("x"), core]).astype(jnp.int32)

    mine, give, tiles = project(
        place, normed, other_normed, cosine, sine, a_blocks, b_blocks
    )
    theirs = swap_cores(give)
    parts = attend(place, mine, theirs, tiles, key_conv)
    merged = merge(exchange(parts, GROUP), queries, new_kv[0])
    attended = exchange(merged, GROUP)[:, :heads].reshape(groups, local_width)
    decoded = jnp.dot(attended, out_weight, preferred_element_type=jnp.float32)
    tp = lax.axis_size("tp")
    decoded = exchange(decoded.reshape(tp, groups // tp, -1), "tp")
    decoded = jnp.sum(decoded, axis=0).astype(jnp.bfloat16)

    keys = jnp.where(first_core, mine, theirs)
    values = jnp.where(first_core, theirs, mine)
    kv_cache = jnp.stack([keys, values], axis=1).reshape(slot_dev, block_rows, 2, local_width)
    return (kv_cache, decoded)


def solution(mesh):
    groups, tp = mesh.devices.shape
    fine = Mesh(
        mesh.devices.reshape(Z_CHIPS, X_CHIPS, groups // (Z_CHIPS * X_CHIPS), tp), GROUP + ("tp",)
    )
    placed = (
        P(GROUP, None, None),
        P(GROUP),
        P(),
        P(),
        P(GROUP, None, "tp"),
        P("tp", GROUP),
        P(GROUP, "tp"),
        P(GROUP, None, "tp"),
        P(GROUP),
    )
    return jax.shard_map(
        per_device,
        mesh=fine,
        in_specs=placed,
        out_specs=(P(GROUP, None, None, "tp"), P("tp", GROUP)),
        check_vma=False,
    )
```
